256 devices in a mesh: gx: 4 (over z_hi, core), gy: 4 (over z_lo), gz: 16 (over y, x).
Axes of the slice: x: 4, y: 4, z: 8 (z_hi: 2, z_lo: 4; z = z_hi * 4 + z_lo), core: 2. Of those that a mesh axis runs over, the one named last changes fastest.
Arguments:
- observed: float32 [512, 128, 512], P('gz', 'gx', 'gy'), may hold values from 0.25 to 4
- profile_x: float32 [31], replicated, may hold values from 0.05 to 1
- profile_y: float32 [31], replicated, may hold values from 0.05 to 1
- profile_z: float32 [61], replicated, may hold values from 0.05 to 1
Outputs:
- estimate: float32 [512, 128, 512], P('gz', 'gx', 'gy')
- level_two: float32 [64, 256, 256], P('gx', ('gy', 'gz'))
- level_four: float32 [32, 128, 128], P('gx', ('gy', 'gz'))
- level_eight: float32 [16, 64, 64], P('gx', ('gy', 'gz'))
The draws below stay inside these ranges and needn't reach their ends.
All inputs are finite; a program needn't handle non-finite values.
Results may differ from the reference program's by a relative error of at most 0.0001.
Values sent between devices are 32-bit elements; how exact they have to be, the bound alone decides.
A program may use at most 128 MiB of HBM per device.

```python
import math
import jax
import jax.numpy as jnp
from jax import lax

TAPS_X = 31
TAPS_Y = 31
TAPS_Z = 61
ITERS = 2
BX = 32
BY = 128
BZ = 32
NX = 128
NY = 512
NZ = 512


def draw_observed(key, part):
    key = jax.random.fold_in(key, 11)
    dims = (NZ, NX, NY)
    rough = jax.random.uniform(key, dims, jnp.float32, math.log(0.25), math.log(4.0))
    values = jnp.exp(rough)
    return jnp.clip(values, 0.25, 4.0).astype(jnp.float32)


def setup_inputs(seed: int = 0) -> dict:
    keys = jax.random.split(jax.random.key(seed), 5)
    return {
        "observed": draw_observed(jax.random.fold_in(keys[4], 71), 0),
        "profile_x": jnp.clip(jnp.exp(jax.random.uniform(keys[1], (TAPS_X,), jnp.float32, math.log(0.05), math.log(1.0))), 0.05, 1.0),
        "profile_y": jnp.clip(jnp.exp(jax.random.uniform(keys[2], (TAPS_Y,), jnp.float32, math.log(0.05), math.log(1.0))), 0.05, 1.0),
        "profile_z": jnp.clip(jnp.exp(jax.random.uniform(keys[3], (TAPS_Z,), jnp.float32, math.log(0.05), math.log(1.0))), 0.05, 1.0),
    }


def band_matrix(kernel, row_count, col_count, offset, adjoint):
    tap_count = kernel.shape[0]
    half = (tap_count - 1) // 2
    rowsidx = jnp.arange(row_count)[:, None]
    colsidx = jnp.arange(col_count)[None, :]
    if adjoint:
        which = colsidx + half + offset - rowsidx
    else:
        which = rowsidx - offset - colsidx + half
    inside = (which >= 0) & (which < tap_count)
    picked = kernel[jnp.clip(which, 0, tap_count - 1)]
    return jnp.where(inside, picked, 0.0)


def blur_last(field, kernel, block, adjoint):
    length = field.shape[-1]
    count_blocks = length // block
    padded = jnp.pad(field, [(0, 0)] * (field.ndim - 1) + [(block, block)])
    blocks = padded.reshape(field.shape[:-1] + (count_blocks + 2, block))
    matrix = band_matrix(kernel, 3 * block, block, block, adjoint)
    result = None
    for offset_block in range(3):
        term = jnp.einsum("...jr,rc->...jc", blocks[..., offset_block:offset_block + count_blocks, :],
                          matrix[offset_block * block:(offset_block + 1) * block],
                          precision=lax.Precision.HIGHEST)
        result = term if result is None else result + term
    return result.reshape(field.shape)


def blur_axis(field, kernel, axis, block, adjoint):
    moved = jnp.moveaxis(field, axis, -1)
    return jnp.moveaxis(blur_last(moved, kernel, block, adjoint), -1, axis)


def pool_half(field):
    sx, sy, sz = field.shape
    return field.reshape(sx // 2, 2, sy // 2, 2, sz // 2, 2).mean(axis=(1, 3, 5))


def reference(observed, profile_x, profile_y, profile_z):
    kernel_x = profile_x / jnp.sum(profile_x)
    kernel_y = profile_y / jnp.sum(profile_y)
    kernel_z = profile_z / jnp.sum(profile_z)
    estimate = observed
    for step in range(ITERS):
        blurred = blur_axis(estimate, kernel_x, 1, BX, False)
        blurred = blur_axis(blurred, kernel_y, 2, BY, False)
        blurred = blur_axis(blurred, kernel_z, 0, BZ, False)
        ratio = observed / blurred
        correction = blur_axis(ratio, kernel_z, 0, BZ, True)
        correction = blur_axis(correction, kernel_y, 2, BY, True)
        correction = blur_axis(correction, kernel_x, 1, BX, True)
        estimate = estimate * correction
    level_two = pool_half(jnp.transpose(estimate, (1, 2, 0)))
    level_four = pool_half(level_two)
    level_eight = pool_half(level_four)
    return estimate, level_two, level_four, level_eight
```

```python
import functools

import jax
import jax.numpy as jnp
from jax import lax
from jax.experimental import pallas as pl
from jax.experimental.pallas import tpu as pltpu
from jax.sharding import PartitionSpec as P

MESH = pl.DeviceIdType.MESH
F32, BF16 = jnp.float32, jnp.bfloat16
CHUNKS = 4
TILES = 4 // CHUNKS
DEPTH = 32 // CHUNKS


def split(value):
    high = value.astype(BF16)
    return high, (value - high.astype(F32)).astype(BF16)


def dot(a, b):
    return jnp.dot(a, b, preferred_element_type=F32)


def left_product(matrix, value):
    high, low = split(value)
    return dot(matrix[0], high) + (dot(matrix[1], high) + dot(matrix[0], low))


def right_product(value, matrix):
    high, low = split(value)
    return dot(high, matrix[0]) + (dot(high, matrix[1]) + dot(low, matrix[0]))


def toeplitz(taps, count, rows, width, first, step):
    lane = lax.broadcasted_iota(jnp.int32, (8, width), 1)
    base = jnp.zeros((8, width), F32)
    total = taps[0]
    for s in range(count):
        base = jnp.where(lane == first + step * s, taps[s], base)
        if s:
            total = total + taps[s]
    base = base / jnp.full((8, width), total, F32)
    spread = jnp.broadcast_to(base[0:1], (rows, width))
    return pltpu.roll(spread, 0, 1, stride=1, stride_axis=0)


def store_split(ref, value):
    high, low = split(value)
    ref[0] = high
    ref[1] = low


def y_matrix(ref, taps, first, step):
    full = toeplitz(taps, 31, 256, 256, first, step)[:, 0:128]
    high, low = split(full)
    for i, part in enumerate((high, low)):
        ref[i, 0:128] = part[16:144]
        ref[i, 128:144] = part[0:16]
        ref[i, 144:160] = part[144:160]
        ref[i, 160:256] = jnp.zeros((96, 128), BF16)


def pack_edges(value):
    lane = lax.broadcasted_iota(jnp.int32, (32, 128), 1) // 16
    upper, lower = None, None
    for k in range(8):
        rows = value[32 * k:32 * k + 32]
        up = pltpu.roll(rows, (16 * k + 16) % 128, 1)
        down = pltpu.roll(rows, 16 * k, 1) if k else rows
        upper = up if upper is None else jnp.where(lane == k, up, upper)
        lower = down if lower is None else jnp.where(lane == k, down, lower)
    return upper, lower


def unpack_edges(left, right):
    lane = lax.broadcasted_iota(jnp.int32, (32, 128), 1)
    rows = []
    for k in range(8):
        a = pltpu.roll(left, (128 - 16 * k) % 128, 1) if k else left
        b = pltpu.roll(right, (128 - 16 * k + 16) % 128, 1)
        rows.append(jnp.where(lane < 16, a, b))
    return jnp.concatenate(rows, axis=0)


def kernel(obs_ref, px, py, pz, est_ref, two_ref, four_ref, eight_ref,
           xf, xa, yf, ya, zf, za, obsx, obsb, u, v, zb, rb, wb, w, wyx0, wyx1, est2, est3,
           yfs, yfr, yas, yar, pooled_z, pooled_t, sent_two, got_two, part_four,
           sx_s, sx_r, sy_s, sy_r, sa_s, sa_r, so_s, so_r, sp_s, sp_r):
    gx, gy, gz = lax.axis_index("gx"), lax.axis_index("gy"), lax.axis_index("gz")
    x_sides = ((gx > 0, {"gx": gx - 1}), (gx < 3, {"gx": gx + 1}))
    y_sides = ((gy > 0, {"gy": gy - 1}), (gy < 3, {"gy": gy + 1}))

    obsx[0:16] = jnp.zeros((16, 32, 128), F32)
    obsx[48:64] = jnp.zeros((16, 32, 128), F32)
    for t in range(2):
        for j in range(2):
            zb[t, j, 0:64] = jnp.zeros((64, 128), F32)
            zb[t, j, 576:640] = jnp.zeros((64, 128), F32)
        for side in range(2):
            yfr[t, side] = jnp.zeros((128, 128), F32)
            yar[t, side] = jnp.zeros((128, 128), F32)
    for j in range(2):
        rb[j, 0:64] = jnp.zeros((64, 128), F32)
        rb[j, 576:640] = jnp.zeros((64, 128), F32)
    wyx0[0:32] = jnp.zeros((32, 32, 128), F32)
    wyx0[64:96] = jnp.zeros((32, 32, 128), F32)
    wyx1[0:16] = jnp.zeros((16, 32, 128), F32)
    wyx1[48:64] = jnp.zeros((16, 32, 128), F32)

    barrier = pltpu.get_barrier_semaphore()

    def greet(k, carry):
        pl.semaphore_signal(barrier, inc=1, device_id={"gz": lax.rem(gz + k, 16)}, device_id_type=MESH)
        return carry

    lax.fori_loop(1, 16, greet, 0)
    for there, target in x_sides + y_sides:
        @pl.when(there)
        def _():
            pl.semaphore_signal(barrier, inc=1, device_id=target, device_id_type=MESH)

    for x in range(32):
        obsx[16 + x] = obs_ref[pl.ds(x, 32, stride=32), :]
    store_split(xf, toeplitz(px, 31, 256, 512, 8, 8))

    neighbours = sum(there.astype(jnp.int32) for there, _ in x_sides + y_sides)
    pl.semaphore_wait(barrier, 15 + neighbours)

    def x_copy(phase, side, c):
        z = pl.ds(DEPTH * c, DEPTH)
        if phase == 0:
            buffer, own, width, low, high = obsx, 16, 15, 1, 48
        elif phase == 1:
            buffer, own, width, low, high = wyx0, 32, 30, 2, 64
        else:
            buffer, own, width, low, high = wyx1, 16, 15, 1, 48
        source = own if side == 0 else own + 32 - width
        target = high if side == 0 else low
        return pltpu.make_async_remote_copy(
            src_ref=buffer.at[pl.ds(source, width), z], dst_ref=buffer.at[pl.ds(target, width), z],
            send_sem=sx_s.at[phase, side, c], recv_sem=sx_r.at[phase, side, c],
            device_id=x_sides[side][1], device_id_type=MESH)

    def y_copy(phase, side, c):
        t = phase // 2
        sent, got = (yfs, yfr) if phase % 2 == 0 else (yas, yar)
        rows = pl.ds(32 * TILES * c, 32 * TILES)
        return pltpu.make_async_remote_copy(
            src_ref=sent.at[t, side, rows], dst_ref=got.at[t, 1 - side, rows],
            send_sem=sy_s.at[phase, side, c], recv_sem=sy_r.at[phase, 1 - side, c],
            device_id=y_sides[side][1], device_id_type=MESH)

    def start(sides, copy, phase, c):
        for side in range(2):
            @pl.when(sides[side][0])
            def _():
                copy(phase, side, c).start()

    def arrive(sides, copy, phase, c):
        for side in range(2):
            @pl.when(sides[side][0])
            def _():
                copy(phase, 1 - side, c).wait_recv()

    def depart(sides, copy, phase, c):
        for side in range(2):
            @pl.when(sides[side][0])
            def _():
                copy(phase, side, c).wait_send()

    def everyone(source, target, send_sem, recv_sem):
        def one(k, carry):
            d = lax.rem(gz + k, 16)
            pltpu.make_async_remote_copy(
                src_ref=source(d), dst_ref=target, send_sem=send_sem, recv_sem=recv_sem,
                device_id={"gz": d}, device_id_type=MESH).start()
            return carry
        lax.fori_loop(1, 16, one, 0)

    def await_bytes(ref, sem):
        pltpu.make_async_copy(ref, ref, sem).wait()

    def columns(ref, first, count, c):
        parts = [ref[first:first + count, DEPTH * c + 8 * j:DEPTH * c + 8 * j + 8, :].reshape(8 * count, 128)
                 for j in range(TILES)]
        return parts[0] if TILES == 1 else jnp.concatenate(parts, axis=1)

    def tile(value, j):
        return value[:, 128 * j:128 * j + 128]

    def pack_and_send(value, phase, c):
        t = phase // 2
        sent = yfs if phase % 2 == 0 else yas
        for j in range(TILES):
            upper, lower = pack_edges(tile(value, j))
            rows = slice(32 * (TILES * c + j), 32 * (TILES * c + j) + 32)
            sent[t, 0, rows] = lower
            sent[t, 1, rows] = upper
        start(y_sides, y_copy, phase, c)

    def blur_y(source, phase, c, matrix, target, first):
        t = phase // 2
        got = yfr if phase % 2 == 0 else yar
        arrive(y_sides, y_copy, phase, c)
        for j in range(TILES):
            z = slice(DEPTH * c + 8 * j, DEPTH * c + 8 * j + 8)
            rows = slice(32 * (TILES * c + j), 32 * (TILES * c + j) + 32)
            halo = unpack_edges(got[t, 0, rows], got[t, 1, rows])
            own = source[:, z, :].reshape(256, 128)
            result = right_product(jnp.concatenate([own, halo], axis=1), matrix)
            target[first:first + 32, z, :] = result.reshape(32, 8, 128)

    def forward_end(t, c):
        blur_y(u, 2 * t, c, yf, v.at[t], 0)
        z = pl.ds(DEPTH * c, DEPTH)
        place = pl.ds(pl.multiple_of(64 + 32 * gz + DEPTH * c, 8), DEPTH)
        everyone(lambda d: v.at[t, pl.ds(2 * d, 2), z], zb.at[t, :, place], sa_s.at[t, 0], sa_r.at[t, 0])
        zb[t, :, place, :] = v[t, pl.ds(2 * gz, 2), z, :]

    def blur_x(matrix, ref, first, c):
        return left_product(matrix, columns(ref, first, 64, c))

    def store_columns(ref, first, value, c):
        for j in range(TILES):
            z = slice(DEPTH * c + 8 * j, DEPTH * c + 8 * j + 8)
            ref[first:first + 32, z, :] = tile(value, j).reshape(32, 8, 128)

    def middle(t):
        await_bytes(zb.at[t, :, pl.ds(0, 480)], sa_r.at[t, 0])
        for b in range(4):
            window = jnp.concatenate([zb[t, j, 128 * b:128 * b + 256, :] for j in range(2)], axis=1)
            blurred = left_product(zf, window)
            for j in range(2):
                rb[j, 64 + 128 * b:192 + 128 * b] = obsb[j, 128 * b:128 * b + 128, :] / tile(blurred, j)
        for b in range(4):
            window = jnp.concatenate([rb[j, 128 * b:128 * b + 256, :] for j in range(2)], axis=1)
            back = left_product(za, window)
            for j in range(2):
                wb[t, j, 128 * b:128 * b + 128] = tile(back, j)
        mine = pl.ds(2 * gz, 2)
        for c in range(CHUNKS):
            everyone(lambda d: wb.at[t, :, pl.ds(pl.multiple_of(32 * d + DEPTH * c, 8), DEPTH)],
                     w.at[t, mine, pl.ds(DEPTH * c, DEPTH)], sa_s.at[t, 1], sa_r.at[t, 1 + c])
        w[t, mine] = wb[t, :, pl.ds(pl.multiple_of(32 * gz, 8), 32), :]

    def back_y(t, c):
        await_bytes(w.at[t, pl.ds(0, 30), pl.ds(0, DEPTH)], sa_r.at[t, 1 + c])
        pack_and_send(columns(w.at[t], 0, 32, c), 2 * t + 1, c)

    for c in range(CHUNKS):
        start(x_sides, x_copy, 0, c)
    everyone(lambda d: obsx.at[pl.ds(16 + 2 * d, 2)], obsb.at[:, pl.ds(pl.multiple_of(32 * gz, 8), 32)],
             so_s, so_r)
    obsb[:, pl.ds(pl.multiple_of(32 * gz, 8), 32), :] = obsx[pl.ds(16 + 2 * gz, 2)]
    y_matrix(yf, py, 255, -1)
    store_split(zf, toeplitz(pz, 61, 128, 256, 34, 1))
    store_split(za, toeplitz(pz, 61, 128, 256, 94, -1))
    store_split(xa, toeplitz(px, 31, 256, 512, 248, -8))
    y_matrix(ya, py, 225, 1)

    for i in range(CHUNKS + 1):
        if i < CHUNKS:
            arrive(x_sides, x_copy, 0, i)
            value = blur_x(xf, obsx, 0, i)
            store_columns(u, 0, value, i)
            pack_and_send(value, 0, i)
        if i >= 1:
            forward_end(0, i - 1)
    await_bytes(obsb.at[:, pl.ds(0, 480)], so_r)
    middle(0)

    for i in range(CHUNKS + 3):
        if i < CHUNKS:
            back_y(0, i)
        if 0 <= i - 1 < CHUNKS:
            blur_y(w.at[0], 1, i - 1, ya, wyx0, 32)
            start(x_sides, x_copy, 1, i - 1)
        if 0 <= i - 2 < CHUNKS:
            c = i - 2
            arrive(x_sides, x_copy, 1, c)
            for half in range(2):
                correction = blur_x(xa, wyx0, 32 * half, c)
                store_columns(est2, 32 * half, columns(obsx, 32 * half, 32, c) * correction, c)
            value = blur_x(xf, est2, 0, c)
            depart(y_sides, y_copy, 0, c)
            store_columns(u, 0, value, c)
            pack_and_send(value, 2, c)
        if i >= 3:
            forward_end(1, i - 3)
    middle(1)

    for i in range(CHUNKS + 2):
        if i < CHUNKS:
            back_y(1, i)
        if 0 <= i - 1 < CHUNKS:
            blur_y(w.at[1], 3, i - 1, ya, wyx1, 16)
            start(x_sides, x_copy, 2, i - 1)
        if i >= 2:
            c = i - 2
            arrive(x_sides, x_copy, 2, c)
            correction = blur_x(xa, wyx1, 0, c)
            for j in range(TILES):
                z = slice(DEPTH * c + 8 * j, DEPTH * c + 8 * j + 8)
                new = est2[16:48, z, :] * tile(correction, j).reshape(32, 8, 128)
                for x in range(32):
                    est3[32 * x + z.start:32 * x + z.stop] = new[x]
                for x in range(16):
                    pooled_z[32 * x + z.start:32 * x + z.stop] = new[2 * x] + new[2 * x + 1]

    halves = pooled_z[pl.ds(0, 256, stride=2), :] + pooled_z[pl.ds(1, 256, stride=2), :]
    for half in range(2):
        pooled_t[half] = jnp.transpose(halves[128 * half:128 * half + 128])
        even, odd = pooled_t[half, pl.ds(0, 64, stride=2), :], pooled_t[half, pl.ds(1, 64, stride=2), :]
        level = (even + odd) * 0.125
        for d in range(16):
            sent_two[d, 4 * half:4 * half + 4] = level[4 * d:4 * d + 4]
    everyone(lambda d: sent_two.at[d], got_two.at[gz], sp_s, sp_r)
    got_two[gz] = sent_two[gz]
    for z in range(32):
        est_ref[32 * z:32 * z + 32] = est3[pl.ds(z, 32, stride=32), :]
    await_bytes(got_two.at[pl.ds(0, 15)], sp_r)
    group = lax.broadcasted_iota(jnp.int32, (8, 128), 1) // 16
    for half in range(2):
        blocks = [got_two[8 * half + s] for s in range(8)]
        for bit in range(3):
            step = 1 << bit
            upper = (group & step) != 0
            for s in range(8):
                if s & step == 0:
                    a, b = blocks[s], blocks[s + step]
                    blocks[s] = jnp.where(upper, pltpu.roll(b, 16 * step, 1), a)
                    blocks[s + step] = jnp.where(upper, b, pltpu.roll(a, 128 - 16 * step, 1))
        for x in range(8):
            two_ref[x, :, 128 * half:128 * half + 128] = blocks[x][0:4]
            two_ref[8 + x, :, 128 * half:128 * half + 128] = blocks[x][4:8]

    def pool_matrix(rows):
        r = lax.broadcasted_iota(jnp.int32, (rows, rows // 2), 0)
        c = lax.broadcasted_iota(jnp.int32, (rows, rows // 2), 1)
        return jnp.where(r // 2 == c, 0.125, 0.0).astype(F32)

    for a in range(8):
        s = two_ref[2 * a] + two_ref[2 * a + 1]
        part_four[2 * a:2 * a + 1] = s[0:1] + s[1:2]
        part_four[2 * a + 1:2 * a + 2] = s[2:3] + s[3:4]
    four = jnp.dot(part_four[...], pool_matrix(256), precision=lax.Precision.HIGHEST, preferred_element_type=F32)
    for a in range(8):
        four_ref[a] = four[2 * a:2 * a + 2]
    rows = [four[4 * a:4 * a + 1] + four[4 * a + 1:4 * a + 2] + four[4 * a + 2:4 * a + 3] + four[4 * a + 3:4 * a + 4]
            for a in range(4)]
    eight = jnp.dot(jnp.concatenate(rows + rows, axis=0), pool_matrix(128),
                    precision=lax.Precision.HIGHEST, preferred_element_type=F32)
    for a in range(4):
        eight_ref[a] = eight[a:a + 1]

    for c in range(CHUNKS):
        for phase in range(3):
            depart(x_sides, x_copy, phase, c)
        for phase in range(1, 4):
            depart(y_sides, y_copy, phase, c)
    for t in range(2):
        await_bytes(zb.at[t, :, pl.ds(0, 480)], sa_s.at[t, 0])
        await_bytes(wb.at[t, :, pl.ds(0, 480)], sa_s.at[t, 1])
    await_bytes(obsb.at[:, pl.ds(0, 480)], so_s)
    await_bytes(sent_two.at[pl.ds(0, 15)], sp_s)


def shards(observed, profile_x, profile_y, profile_z):
    vmem = pl.BlockSpec(memory_space=pltpu.VMEM)
    smem = pl.BlockSpec(memory_space=pltpu.SMEM)
    dma = pltpu.SemaphoreType.DMA
    estimate, two, four, eight = pl.pallas_call(
        kernel,
        out_shape=[
            jax.ShapeDtypeStruct((1024, 128), F32),
            jax.ShapeDtypeStruct((16, 4, 256), F32),
            jax.ShapeDtypeStruct((8, 2, 128), F32),
            jax.ShapeDtypeStruct((4, 1, 64), F32),
        ],
        in_specs=[vmem, smem, smem, smem],
        out_specs=[vmem] * 4,
        scratch_shapes=[
            pltpu.VMEM((2, 256, 512), BF16),
            pltpu.VMEM((2, 256, 512), BF16),
            pltpu.VMEM((2, 256, 128), BF16),
            pltpu.VMEM((2, 256, 128), BF16),
            pltpu.VMEM((2, 128, 256), BF16),
            pltpu.VMEM((2, 128, 256), BF16),
            pltpu.VMEM((64, 32, 128), F32),
            pltpu.VMEM((2, 512, 128), F32),
            pltpu.VMEM((32, 32, 128), F32),
            pltpu.VMEM((2, 32, 32, 128), F32),
            pltpu.VMEM((2, 2, 640, 128), F32),
            pltpu.VMEM((2, 640, 128), F32),
            pltpu.VMEM((2, 2, 512, 128), F32),
            pltpu.VMEM((2, 32, 32, 128), F32),
            pltpu.VMEM((96, 32, 128), F32),
            pltpu.VMEM((64, 32, 128), F32),
            pltpu.VMEM((64, 32, 128), F32),
            pltpu.VMEM((1024, 128), F32),
            pltpu.VMEM((2, 2, 128, 128), F32),
            pltpu.VMEM((2, 2, 128, 128), F32),
            pltpu.VMEM((2, 2, 128, 128), F32),
            pltpu.VMEM((2, 2, 128, 128), F32),
            pltpu.VMEM((512, 128), F32),
            pltpu.VMEM((2, 128, 128), F32),
            pltpu.VMEM((16, 8, 128), F32),
            pltpu.VMEM((16, 8, 128), F32),
            pltpu.VMEM((16, 256), F32),
            dma((3, 2, CHUNKS)), dma((3, 2, CHUNKS)),
            dma((4, 2, CHUNKS)), dma((4, 2, CHUNKS)),
            dma((2, 2)), dma((2, 1 + CHUNKS)),
            dma, dma, dma, dma,
        ],
        compiler_params=pltpu.CompilerParams(
            collective_id=0, has_side_effects=True, vmem_limit_bytes=48 * 1024 * 1024),
        name="deconvolve",
    )(observed.reshape(1024, 128), profile_x, profile_y, profile_z)
    return estimate.reshape(32, 32, 128), two, four, eight


def solution(mesh):
    return jax.shard_map(
        shards,
        mesh=mesh,
        in_specs=(P("gz", "gx", "gy"), P(), P(), P()),
        out_specs=(
            P("gz", "gx", "gy"),
            P("gx", ("gy", "gz"), None),
            P("gx", ("gy", "gz"), None),
            P("gx", ("gy", "gz"), None),
        ),
        check_vma=False,
    )
```

```python
import functools

import jax
import jax.numpy as jnp
from jax import lax
from jax.experimental import pallas as pl
from jax.experimental.pallas import tpu as pltpu
from jax.sharding import PartitionSpec as P

MESH = pl.DeviceIdType.MESH
F32, BF16 = jnp.float32, jnp.bfloat16
CHUNKS = 2
TILES = 4 // CHUNKS
DEPTH = 32 // CHUNKS


def split(value):
    high = value.astype(BF16)
    return high, (value - high.astype(F32)).astype(BF16)


def dot(a, b):
    return jnp.dot(a, b, preferred_element_type=F32)


def left_product(matrix, value):
    high, low = split(value)
    return dot(matrix[0], high) + (dot(matrix[1], high) + dot(matrix[0], low))


def right_product(value, matrix):
    high, low = split(value)
    return dot(high, matrix[0]) + (dot(high, matrix[1]) + dot(low, matrix[0]))


def toeplitz(taps, count, rows, width, first, step):
    lane = lax.broadcasted_iota(jnp.int32, (8, width), 1)
    base = jnp.zeros((8, width), F32)
    total = taps[0]
    for s in range(count):
        base = jnp.where(lane == first + step * s, taps[s], base)
        if s:
            total = total + taps[s]
    base = base / jnp.full((8, width), total, F32)
    spread = jnp.broadcast_to(base[0:1], (rows, width))
    return pltpu.roll(spread, 0, 1, stride=1, stride_axis=0)


def store_split(ref, value):
    high, low = split(value)
    ref[0] = high
    ref[1] = low


def y_forward(ref, taps):
    full = toeplitz(taps, 31, 256, 256, 255, -1)
    lane = lax.broadcasted_iota(jnp.int32, (256, 128), 1) // 16
    own = pltpu.roll(full, 240, 1)[:, 0:128]
    for j in range(2):
        left = pltpu.roll(full, 16 * j, 1)[:, 0:128] if j else full[:, 0:128]
        right = pltpu.roll(full, 144 + 16 * j, 1)[:, 0:128]
        side = jnp.where(lane == j, left, jnp.where(lane == 2 + j, right, 0.0))
        for i, part in enumerate(split(jnp.concatenate([own, side], axis=1))):
            ref[j, i, 0:128] = part[32:160]
            ref[j, i, 128:160] = part[0:32]
            ref[j, i, 160:192] = part[160:192]
            ref[j, i, 192:256] = jnp.zeros((64, 256), BF16)


def y_adjoint(ref, taps):
    full = toeplitz(taps, 31, 256, 256, 225, 1)[:, 0:128]
    for i, part in enumerate(split(full)):
        for j in range(2):
            ref[j, i, 128:256] = jnp.zeros((128, 128), BF16)
            ref[j, i, 0:128] = part[16:144]
            ref[j, i, 128 + 16 * j:144 + 16 * j] = part[0:16]
            ref[j, i, 160 + 16 * j:176 + 16 * j] = part[144:160]


def gather_lanes(parts, width, first):
    lane = lax.broadcasted_iota(jnp.int32, parts[0].shape, 1) // width
    result = None
    for k, part in enumerate(parts):
        shift = (width * k - first) % 128
        moved = pltpu.roll(part, shift, 1) if shift else part
        result = moved if result is None else jnp.where(lane == k, moved, result)
    return result


def spread_lanes(left, right, width, k):
    lane = lax.broadcasted_iota(jnp.int32, left.shape, 1)
    a, b = (128 - width * k) % 128, (width - width * k) % 128
    left = pltpu.roll(left, a, 1) if a else left
    right = pltpu.roll(right, b, 1) if b else right
    return jnp.where(lane < width, left, right)


def kernel(obs_ref, px, py, pz, est_ref, two_ref, four_ref, eight_ref,
           xf, xa, yf, ya, zf, za, obsx, obsb, obss, obse_s, obse_r, u, um, ue_s, ue_r, zb, rb, wb,
           wyx0, wyx1, est2, est3, pooled_z, pooled_t, sent_two, got_two, part_four,
           sx_s, sx_r, sn_s, sn_r, sf_s, sf_r, se_s, se_r, sa_s, sa_r, so_s, so_r, sp_s, sp_r):
    gx, gy, gz = lax.axis_index("gx"), lax.axis_index("gy"), lax.axis_index("gz")
    x_sides = ((gx > 0, {"gx": gx - 1}), (gx < 3, {"gx": gx + 1}))
    y_sides = ((gy > 0, gy - 1), (gy < 3, gy + 1))
    inner = (gx == 1) | (gx == 2)
    parity = lax.rem(gx, 2)

    obsx[0, 0] = jnp.zeros((32, 128), F32)
    obsx[3, 15] = jnp.zeros((32, 128), F32)

    @pl.when(gx == 0)
    def _():
        obsx[0] = jnp.zeros((16, 32, 128), F32)
        wyx0[0:2] = jnp.zeros((2, 16, 32, 128), F32)
        wyx1[0] = jnp.zeros((16, 32, 128), F32)

    @pl.when(gx == 3)
    def _():
        obsx[3] = jnp.zeros((16, 32, 128), F32)
        wyx0[4:6] = jnp.zeros((2, 16, 32, 128), F32)
        wyx1[3] = jnp.zeros((16, 32, 128), F32)

    for side in range(2):
        @pl.when(jnp.logical_not(y_sides[side][0]))
        def _():
            obse_r[side] = jnp.zeros((16, 8, 128), F32)
            for t in range(2):
                ue_r[t, side] = jnp.zeros((CHUNKS, 16, 8, 128), F32)

    barrier = pltpu.get_barrier_semaphore()

    def greet(target):
        pl.semaphore_signal(barrier, inc=1, device_id=target, device_id_type=MESH)

    def others(body):
        def one(k, carry):
            body(lax.rem(gz + k, 16))
            return carry
        lax.fori_loop(1, 16, one, 0)

    def everyone(body):
        def one(k, carry):
            body(lax.rem(gz + k, 16))
            return carry
        lax.fori_loop(0, 16, one, 0)

    greet({"gx": gx + 1 - 2 * parity})

    @pl.when(inner)
    def _():
        everyone(lambda d: greet({"gx": 3 - gx, "gz": d}))
    others(lambda d: greet({"gz": d}))
    for there, target in y_sides:
        @pl.when(there)
        def _():
            everyone(lambda d: greet({"gy": target, "gz": d}))

    for x in range(32):
        obsx[1 + x // 16, x % 16] = obs_ref[pl.ds(x, 32, stride=32), :]

    neighbours = sum(there.astype(jnp.int32) for there, _ in y_sides) + inner.astype(jnp.int32)
    pl.semaphore_wait(barrier, 16 + 16 * neighbours)

    def await_bytes(ref, sem):
        pltpu.make_async_copy(ref, ref, sem).wait()

    def z_of(c):
        return pl.ds(DEPTH * c, DEPTH)

    def x_copy(side, c):
        source = obsx.at[1, pl.ds(0, 15), z_of(c)] if side == 0 else obsx.at[2, pl.ds(1, 15), z_of(c)]
        target = obsx.at[3, pl.ds(0, 15), z_of(c)] if side == 0 else obsx.at[0, pl.ds(1, 15), z_of(c)]
        return pltpu.make_async_remote_copy(
            src_ref=source, dst_ref=target, send_sem=sx_s.at[side, c], recv_sem=sx_r.at[side, c],
            device_id=x_sides[side][1], device_id_type=MESH)

    for c in range(CHUNKS):
        for side in range(2):
            @pl.when(x_sides[side][0])
            def _():
                x_copy(side, c).start()

    def send(source, target, send_sem, recv_sem, device):
        pltpu.make_async_remote_copy(
            src_ref=source, dst_ref=target, send_sem=send_sem, recv_sem=recv_sem,
            device_id=device, device_id_type=MESH).start()

    others(lambda d: send(obsx.at[pl.ds(1, 2), d], obsb.at[:, gz], so_s, so_r, {"gz": d}))
    obsb[:, gz] = obsx[1:3, gz]
    for side, first in ((0, 0), (1, 112)):
        parts = [obsx[1 + j, :, 8 * k:8 * k + 8, :].reshape(128, 128) for k in range(4) for j in range(2)]
        obse_s[side] = gather_lanes(parts, 16, first).reshape(16, 8, 128)

        @pl.when(y_sides[side][0])
        def _():
            everyone(lambda d: send(obse_s.at[side, d], obse_r.at[1 - side, gz], se_s.at[2, side, 0],
                                    se_r.at[2, 1 - side, 0], {"gy": y_sides[side][1], "gz": d}))

    store_split(xf, toeplitz(px, 31, 256, 512, 8, 8))
    y_forward(yf, py)
    store_split(zf, toeplitz(pz, 61, 128, 256, 34, 1))
    store_split(za, toeplitz(pz, 61, 128, 256, 94, -1))
    store_split(xa, toeplitz(px, 31, 256, 512, 248, -8))
    y_adjoint(ya, py)
    for part in range(3):
        for ref in (zb, rb):
            ref[part, 0:2] = jnp.zeros((2, 32, 128), F32)
            ref[part, 18:20] = jnp.zeros((2, 32, 128), F32)

    def columns(ref, first, count, c):
        parts = [ref[first:first + count, :, DEPTH * c + 8 * j:DEPTH * c + 8 * j + 8, :].reshape(128 * count, 128)
                 for j in range(TILES)]
        return parts[0] if TILES == 1 else jnp.concatenate(parts, axis=1)

    def tile(value, j):
        return value[:, 128 * j:128 * j + 128]

    def blur_x(matrix, ref, first, c):
        return left_product(matrix, columns(ref, first, 4, c))

    def store_columns(ref, first, value, c):
        for j in range(TILES):
            z = slice(DEPTH * c + 8 * j, DEPTH * c + 8 * j + 8)
            ref[first:first + 2, :, z, :] = tile(value, j).reshape(2, 16, 8, 128)

    def to_columns(t, value, c):
        store_columns(u.at[t], 0, value, c)
        others(lambda d: send(u.at[t, :, d, z_of(c)], um.at[t, :, gz, z_of(c)], sa_s.at[t, 0], sa_r.at[t, 0, c],
                              {"gz": d}))
        parts = [tile(value, k)[128 * j:128 * j + 128] for k in range(TILES) for j in range(2)]
        for side, first in ((0, 0), (1, 96)):
            ue_s[t, side, c] = gather_lanes(parts, 32, first).reshape(16, 8, 128)

            @pl.when(y_sides[side][0])
            def _():
                everyone(lambda d: send(ue_s.at[t, side, c, d], ue_r.at[t, 1 - side, c, gz], se_s.at[t, side, c],
                                        se_r.at[t, 1 - side, c], {"gy": y_sides[side][1], "gz": d}))
        um[t, :, gz, z_of(c), :] = u[t, :, gz, z_of(c), :]

    def middle(t, own):
        for c in range(CHUNKS):
            await_bytes(um.at[t, :, pl.ds(0, 15), pl.ds(0, DEPTH)], sa_r.at[t, 0, c])
            for side in range(2):
                @pl.when(y_sides[side][0])
                def _():
                    await_bytes(ue_r.at[t, side, c], se_r.at[t, side, c])
            left, right = (ue_r[t, side, c].reshape(128, 128) for side in range(2))
            sides = None
            for j in range(2):
                halo = jnp.concatenate(
                    [spread_lanes(left, right, 32, 2 * k + j).reshape(16, 8, 128) for k in range(TILES)], axis=1)
                own_lanes = um[t, j, :, DEPTH * c:DEPTH * c + DEPTH, :].reshape(16 * DEPTH, 128)
                result = right_product(jnp.concatenate([own_lanes, halo.reshape(16 * DEPTH, 128)], axis=1), yf.at[j])
                zb[j, 2:18, DEPTH * c:DEPTH * c + DEPTH, :] = tile(result, 0).reshape(16, DEPTH, 128)
                sides = tile(result, 1) if sides is None else sides + tile(result, 1)
            zb[2, 2:18, DEPTH * c:DEPTH * c + DEPTH, :] = sides.reshape(16, DEPTH, 128)
        if t == 0:
            await_bytes(obsb.at[:, pl.ds(0, 15)], so_r)
            for side in range(2):
                @pl.when(y_sides[side][0])
                def _():
                    await_bytes(obse_r.at[side], se_r.at[2, side, 0])
            left, right = (obse_r[side].reshape(128, 128) for side in range(2))
            lane = lax.broadcasted_iota(jnp.int32, (128, 128), 1)
            for k in range(4):
                part = spread_lanes(left, right, 32, k)
                obss[:, 8 * k:8 * k + 8, :] = jnp.where(lane < 64, part, 0.0).reshape(16, 8, 128)
        lane = lax.broadcasted_iota(jnp.int32, (128, 128), 1)
        inside = ((lane < 32) & (gy > 0)) | ((lane >= 32) & (lane < 64) & (gy < 3))
        for b in range(4):
            window = jnp.concatenate([zb[j, 4 * b:4 * b + 8].reshape(256, 128) for j in range(3)], axis=1)
            blurred = left_product(zf, window)
            for j in range(2):
                ratio = obsb[j, 4 * b:4 * b + 4].reshape(128, 128) / tile(blurred, j)
                rb[j, 2 + 4 * b:6 + 4 * b] = ratio.reshape(4, 32, 128)
            ratio = obss[4 * b:4 * b + 4].reshape(128, 128) / jnp.where(inside, tile(blurred, 2), 1.0)
            rb[2, 2 + 4 * b:6 + 4 * b] = jnp.where(inside, ratio, 0.0).reshape(4, 32, 128)
        for b in range(4):
            window = jnp.concatenate([rb[j, 4 * b:4 * b + 8].reshape(256, 128) for j in range(3)], axis=1)
            back = left_product(za, window)
            for j in range(2):
                result = right_product(jnp.concatenate([tile(back, j), tile(back, 2)], axis=1), ya.at[j])
                wb[t, j, 4 * b:4 * b + 4] = result.reshape(4, 32, 128)
        for c in range(CHUNKS):
            @pl.when(inner)
            def _():
                if t == 0:
                    first = 4 * (gx - 1)
                    everyone(lambda d: send(wb.at[t, :, d, z_of(c)], own.at[pl.ds(first, 2), gz, z_of(c)],
                                            sf_s.at[t], sf_r.at[t, c], {"gx": 3 - gx, "gz": d}))
                else:
                    first = 3 * (gx - 1)
                    everyone(lambda d: send(wb.at[t, 2 - gx, d, z_of(c)], own.at[first, gz, z_of(c)],
                                            sf_s.at[t], sf_r.at[t, c], {"gx": 3 - gx, "gz": d}))
            others(lambda d: send(wb.at[t, :, d, z_of(c)], own.at[pl.ds(2 - t, 2), gz, z_of(c)],
                                  sa_s.at[t, 1], sa_r.at[t, 1, c], {"gz": d}))
        own[2 - t:4 - t, gz] = wb[t, :, gz]

    def near_copy(t, ref, c):
        if t == 0:
            source, target = ref.at[pl.ds(2, 2), :, z_of(c)], ref.at[pl.ds(4 * parity, 2), :, z_of(c)]
        else:
            source, target = ref.at[2 - parity, :, z_of(c)], ref.at[3 * parity, :, z_of(c)]
        return pltpu.make_async_remote_copy(
            src_ref=source, dst_ref=target, send_sem=sn_s.at[t, c], recv_sem=sn_r.at[t, c],
            device_id={"gx": gx + 1 - 2 * parity}, device_id_type=MESH)

    def arrive_own(t, ref, c):
        await_bytes(ref.at[pl.ds(2 - t, 2), pl.ds(0, 15), pl.ds(0, DEPTH)], sa_r.at[t, 1, c])
        near_copy(t, ref, c).start()

    def arrive_halos(t, ref, c):
        near_copy(t, ref, c).wait_recv()

        @pl.when(inner)
        def _():
            await_bytes(ref.at[pl.ds(0, 2 - t), :, pl.ds(0, DEPTH)], sf_r.at[t, c])

    for c in range(CHUNKS):
        for side in range(2):
            @pl.when(x_sides[side][0])
            def _():
                x_copy(1 - side, c).wait_recv()
        to_columns(0, blur_x(xf, obsx, 0, c), c)
    middle(0, wyx0)

    for c in range(CHUNKS):
        arrive_own(0, wyx0, c)
    for c in range(CHUNKS):
        arrive_halos(0, wyx0, c)
        for half in range(2):
            correction = blur_x(xa, wyx0, 2 * half, c)
            store_columns(est2, 2 * half, columns(obsx, 2 * half, 2, c) * correction, c)
        to_columns(1, blur_x(xf, est2, 0, c), c)
    middle(1, wyx1)

    for c in range(CHUNKS):
        arrive_own(1, wyx1, c)
    for c in range(CHUNKS):
        arrive_halos(1, wyx1, c)
        correction = blur_x(xa, wyx1, 0, c)
        for j in range(TILES):
            z = slice(DEPTH * c + 8 * j, DEPTH * c + 8 * j + 8)
            new = est2[1:3, :, z, :].reshape(32, 8, 128) * tile(correction, j).reshape(32, 8, 128)
            for x in range(32):
                est3[32 * x + z.start:32 * x + z.stop] = new[x]
            for x in range(16):
                pooled_z[32 * x + z.start:32 * x + z.stop] = new[2 * x] + new[2 * x + 1]

    halves = pooled_z[pl.ds(0, 256, stride=2), :] + pooled_z[pl.ds(1, 256, stride=2), :]
    for half in range(2):
        pooled_t[half] = jnp.transpose(halves[128 * half:128 * half + 128])
        even, odd = pooled_t[half, pl.ds(0, 64, stride=2), :], pooled_t[half, pl.ds(1, 64, stride=2), :]
        level = (even + odd) * 0.125
        for d in range(16):
            sent_two[d, 4 * half:4 * half + 4] = level[4 * d:4 * d + 4]
    others(lambda d: send(sent_two.at[d], got_two.at[gz], sp_s, sp_r, {"gz": d}))
    got_two[gz] = sent_two[gz]
    for z in range(32):
        est_ref[32 * z:32 * z + 32] = est3[pl.ds(z, 32, stride=32), :]
    await_bytes(got_two.at[pl.ds(0, 15)], sp_r)
    group = lax.broadcasted_iota(jnp.int32, (8, 128), 1) // 16
    for half in range(2):
        blocks = [got_two[8 * half + s] for s in range(8)]
        for bit in range(3):
            step = 1 << bit
            upper = (group & step) != 0
            for s in range(8):
                if s & step == 0:
                    a, b = blocks[s], blocks[s + step]
                    blocks[s] = jnp.where(upper, pltpu.roll(b, 16 * step, 1), a)
                    blocks[s + step] = jnp.where(upper, b, pltpu.roll(a, 128 - 16 * step, 1))
        for x in range(8):
            two_ref[x, :, 128 * half:128 * half + 128] = blocks[x][0:4]
            two_ref[8 + x, :, 128 * half:128 * half + 128] = blocks[x][4:8]

    def pool_matrix(rows):
        r = lax.broadcasted_iota(jnp.int32, (rows, rows // 2), 0)
        c = lax.broadcasted_iota(jnp.int32, (rows, rows // 2), 1)
        return jnp.where(r // 2 == c, 0.125, 0.0).astype(F32)

    for a in range(8):
        s = two_ref[2 * a] + two_ref[2 * a + 1]
        part_four[2 * a:2 * a + 1] = s[0:1] + s[1:2]
        part_four[2 * a + 1:2 * a + 2] = s[2:3] + s[3:4]
    four = jnp.dot(part_four[...], pool_matrix(256), precision=lax.Precision.HIGHEST, preferred_element_type=F32)
    for a in range(8):
        four_ref[a] = four[2 * a:2 * a + 2]
    rows = [four[4 * a:4 * a + 1] + four[4 * a + 1:4 * a + 2] + four[4 * a + 2:4 * a + 3] + four[4 * a + 3:4 * a + 4]
            for a in range(4)]
    eight = jnp.dot(jnp.concatenate(rows + rows, axis=0), pool_matrix(128),
                    precision=lax.Precision.HIGHEST, preferred_element_type=F32)
    for a in range(4):
        eight_ref[a] = eight[a:a + 1]

    for c in range(CHUNKS):
        for side in range(2):
            @pl.when(x_sides[side][0])
            def _():
                x_copy(side, c).wait_send()

            @pl.when(y_sides[side][0])
            def _():
                for t in range(2):
                    await_bytes(ue_s.at[t, side, c], se_s.at[t, side, c])
        near_copy(0, wyx0, c).wait_send()
        near_copy(1, wyx1, c).wait_send()
    for side in range(2):
        @pl.when(y_sides[side][0])
        def _():
            await_bytes(obse_s.at[side], se_s.at[2, side, 0])

    @pl.when(inner)
    def _():
        await_bytes(wb.at[0], sf_s.at[0])
        await_bytes(wb.at[1, 0], sf_s.at[1])
    for t in range(2):
        for way in range(2):
            await_bytes(wb.at[t, :, pl.ds(0, 15)], sa_s.at[t, way])
    await_bytes(obsb.at[:, pl.ds(0, 15)], so_s)
    await_bytes(sent_two.at[pl.ds(0, 15)], sp_s)


def shards(observed, profile_x, profile_y, profile_z):
    vmem = pl.BlockSpec(memory_space=pltpu.VMEM)
    smem = pl.BlockSpec(memory_space=pltpu.SMEM)
    dma = pltpu.SemaphoreType.DMA
    estimate, two, four, eight = pl.pallas_call(
        kernel,
        out_shape=[
            jax.ShapeDtypeStruct((1024, 128), F32),
            jax.ShapeDtypeStruct((16, 4, 256), F32),
            jax.ShapeDtypeStruct((8, 2, 128), F32),
            jax.ShapeDtypeStruct((4, 1, 64), F32),
        ],
        in_specs=[vmem, smem, smem, smem],
        out_specs=[vmem] * 4,
        scratch_shapes=[
            pltpu.VMEM((2, 256, 512), BF16),
            pltpu.VMEM((2, 256, 512), BF16),
            pltpu.VMEM((2, 2, 256, 256), BF16),
            pltpu.VMEM((2, 2, 256, 128), BF16),
            pltpu.VMEM((2, 128, 256), BF16),
            pltpu.VMEM((2, 128, 256), BF16),
            pltpu.VMEM((4, 16, 32, 128), F32),
            pltpu.VMEM((2, 16, 32, 128), F32),
            pltpu.VMEM((16, 32, 128), F32),
            pltpu.VMEM((2, 16, 8, 128), F32),
            pltpu.VMEM((2, 16, 8, 128), F32),
            pltpu.VMEM((2, 2, 16, 32, 128), F32),
            pltpu.VMEM((2, 2, 16, 32, 128), F32),
            pltpu.VMEM((2, 2, CHUNKS, 16, 8, 128), F32),
            pltpu.VMEM((2, 2, CHUNKS, 16, 8, 128), F32),
            pltpu.VMEM((3, 20, 32, 128), F32),
            pltpu.VMEM((3, 20, 32, 128), F32),
            pltpu.VMEM((2, 2, 16, 32, 128), F32),
            pltpu.VMEM((6, 16, 32, 128), F32),
            pltpu.VMEM((4, 16, 32, 128), F32),
            pltpu.VMEM((4, 16, 32, 128), F32),
            pltpu.VMEM((1024, 128), F32),
            pltpu.VMEM((512, 128), F32),
            pltpu.VMEM((2, 128, 128), F32),
            pltpu.VMEM((16, 8, 128), F32),
            pltpu.VMEM((16, 8, 128), F32),
            pltpu.VMEM((16, 256), F32),
            dma((2, CHUNKS)), dma((2, CHUNKS)),
            dma((2, CHUNKS)), dma((2, CHUNKS)),
            dma((2,)), dma((2, CHUNKS)),
            dma((3, 2, CHUNKS)), dma((3, 2, CHUNKS)),
            dma((2, 2)), dma((2, 2, CHUNKS)),
            dma, dma, dma, dma,
        ],
        compiler_params=pltpu.CompilerParams(
            collective_id=0, has_side_effects=True, vmem_limit_bytes=48 * 1024 * 1024),
        name="deconvolve",
    )(observed.reshape(1024, 128), profile_x, profile_y, profile_z)
    return estimate.reshape(32, 32, 128), two, four, eight


def solution(mesh):
    return jax.shard_map(
        shards,
        mesh=mesh,
        in_specs=(P("gz", "gx", "gy"), P(), P(), P()),
        out_specs=(
            P("gz", "gx", "gy"),
            P("gx", ("gy", "gz"), None),
            P("gx", ("gy", "gz"), None),
            P("gx", ("gy", "gz"), None),
        ),
        check_vma=False,
    )
```

```python
import functools

import jax
import jax.numpy as jnp
from jax import lax
from jax.experimental import pallas as pl
from jax.experimental.pallas import tpu as pltpu
from jax.sharding import PartitionSpec as P

MESH = pl.DeviceIdType.MESH
F32, BF16 = jnp.float32, jnp.bfloat16
CHUNKS = 2
DEPTH = 32 // CHUNKS
TILES = DEPTH // 8


def split(value):
    high = value.astype(BF16)
    return high, (value - high.astype(F32)).astype(BF16)


def dot(a, b):
    return jnp.dot(a, b, preferred_element_type=F32)


def left_product(matrix, value):
    high, low = split(value)
    return dot(matrix[0], high) + (dot(matrix[1], high) + dot(matrix[0], low))


def right_product(value, matrix):
    high, low = split(value)
    return dot(high, matrix[0]) + (dot(high, matrix[1]) + dot(low, matrix[0]))


def toeplitz(taps, count, rows, width, first, step):
    lane = lax.broadcasted_iota(jnp.int32, (8, width), 1)
    base = jnp.zeros((8, width), F32)
    total = taps[0]
    for s in range(count):
        base = jnp.where(lane == first + step * s, taps[s], base)
        if s:
            total = total + taps[s]
    base = base / jnp.full((8, width), total, F32)
    spread = jnp.broadcast_to(base[0:1], (rows, width))
    return pltpu.roll(spread, 0, 1, stride=1, stride_axis=0)


def store_split(ref, value):
    high, low = split(value)
    ref[0] = high
    ref[1] = low


def y_forward(ref, taps):
    full = toeplitz(taps, 31, 256, 256, 255, -1)
    lane = lax.broadcasted_iota(jnp.int32, (256, 128), 1) // 16
    own = pltpu.roll(full, 240, 1)[:, 0:128]
    for j in range(2):
        left = pltpu.roll(full, 16 * j, 1)[:, 0:128] if j else full[:, 0:128]
        right = pltpu.roll(full, 144 + 16 * j, 1)[:, 0:128]
        side = jnp.where(lane == j, left, jnp.where(lane == 2 + j, right, 0.0))
        for i, part in enumerate(split(jnp.concatenate([own, side], axis=1))):
            ref[j, i, 0:128] = part[32:160]
            ref[j, i, 128:160] = part[0:32]
            ref[j, i, 160:192] = part[160:192]
            ref[j, i, 192:256] = jnp.zeros((64, 256), BF16)


def y_adjoint(ref, taps):
    full = toeplitz(taps, 31, 256, 256, 225, 1)[:, 0:128]
    for i, part in enumerate(split(full)):
        for j in range(2):
            ref[j, i, 128:256] = jnp.zeros((128, 128), BF16)
            ref[j, i, 0:128] = part[16:144]
            ref[j, i, 128 + 16 * j:144 + 16 * j] = part[0:16]
            ref[j, i, 160 + 16 * j:176 + 16 * j] = part[144:160]


def gather_lanes(parts, width, first):
    lane = lax.broadcasted_iota(jnp.int32, parts[0].shape, 1) // width
    result = None
    for k, part in enumerate(parts):
        shift = (width * k - first) % 128
        moved = pltpu.roll(part, shift, 1) if shift else part
        result = moved if result is None else jnp.where(lane == k, moved, result)
    return result


def spread_lanes(left, right, width, k):
    lane = lax.broadcasted_iota(jnp.int32, left.shape, 1)
    a, b = (128 - width * k) % 128, (width - width * k) % 128
    left = pltpu.roll(left, a, 1) if a else left
    right = pltpu.roll(right, b, 1) if b else right
    return jnp.where(lane < width, left, right)


def kernel(obs_hbm, px, py, pz, est_ref, got_two,
           obs_ref, obs_sem, xf, xa, yf, ya, zf, za, obsx, obsb, obss, obse_s, obse_r, u, um, ue_s, ue_r, zb, rb, wb,
           wyx0, wyx1, est2, est3, pooled_z, pooled_t, sent_two,
           sx_s, sx_r, sn_s, sn_r, sf_s, sf_r, se_s, se_r, sa_s, sa_r, so_s, so_r, sp_s, sp_r):
    gx, gy, gz = lax.axis_index("gx"), lax.axis_index("gy"), lax.axis_index("gz")
    x_sides = ((gx > 0, {"gx": gx - 1}), (gx < 3, {"gx": gx + 1}))
    y_sides = ((gy > 0, gy - 1), (gy < 3, gy + 1))
    inner = (gx == 1) | (gx == 2)
    outermost = ((gx == 1) & (gz == 0)) | ((gx == 2) & (gz == 15))
    outer = ((gx == 1) & (gz < 2)) | ((gx == 2) & (gz > 13))
    parity = lax.rem(gx, 2)

    load = pltpu.make_async_copy(obs_hbm, obs_ref, obs_sem)
    load.start()

    obsx[:, 0, 0] = jnp.zeros((CHUNKS, DEPTH, 128), F32)
    obsx[:, 3, 15] = jnp.zeros((CHUNKS, DEPTH, 128), F32)
    wyx0[:, 0:2, 0] = jnp.zeros((CHUNKS, 2, DEPTH, 128), F32)
    wyx0[:, 14:16, 5] = jnp.zeros((CHUNKS, 2, DEPTH, 128), F32)
    wyx1[:, 0, 0] = jnp.zeros((CHUNKS, DEPTH, 128), F32)
    wyx1[:, 15, 3] = jnp.zeros((CHUNKS, DEPTH, 128), F32)

    @pl.when(gx == 0)
    def _():
        obsx[:, 0] = jnp.zeros((CHUNKS, 16, DEPTH, 128), F32)
        wyx0[:, :, 0:2] = jnp.zeros((CHUNKS, 16, 2, DEPTH, 128), F32)
        wyx1[:, :, 0] = jnp.zeros((CHUNKS, 16, DEPTH, 128), F32)

    @pl.when(gx == 3)
    def _():
        obsx[:, 3] = jnp.zeros((CHUNKS, 16, DEPTH, 128), F32)
        wyx0[:, :, 4:6] = jnp.zeros((CHUNKS, 16, 2, DEPTH, 128), F32)
        wyx1[:, :, 3] = jnp.zeros((CHUNKS, 16, DEPTH, 128), F32)

    for side in range(2):
        @pl.when(jnp.logical_not(y_sides[side][0]))
        def _():
            obse_r[side] = jnp.zeros((16, 8, 128), F32)
            for t in range(2):
                ue_r[t, side] = jnp.zeros((CHUNKS, 16, 8, 128), F32)

    barrier = pltpu.get_barrier_semaphore()

    def greet(target):
        pl.semaphore_signal(barrier, inc=1, device_id=target, device_id_type=MESH)

    def others(body):
        def one(k, carry):
            body(lax.rem(gz + k, 16))
            return carry
        lax.fori_loop(1, 16, one, 0)

    def everyone(body):
        def one(k, carry):
            body(lax.rem(gz + k, 16))
            return carry
        lax.fori_loop(0, 16, one, 0)

    greet({"gx": gx + 1 - 2 * parity})

    @pl.when(inner)
    def _():
        everyone(lambda d: greet({"gx": 3 - gx, "gz": d}))
    others(lambda d: greet({"gz": d}))
    for there, target in y_sides:
        @pl.when(there)
        def _():
            everyone(lambda d: greet({"gy": target, "gz": d}))

    load.wait()
    for x in range(32):
        row = obs_ref[pl.ds(x, 32, stride=32), :]
        for c in range(CHUNKS):
            obsx[c, 1 + x // 16, x % 16] = row[DEPTH * c:DEPTH * c + DEPTH]

    neighbours = sum(there.astype(jnp.int32) for there, _ in y_sides) + inner.astype(jnp.int32)
    pl.semaphore_wait(barrier, 16 + 16 * neighbours)

    def await_bytes(ref, sem):
        pltpu.make_async_copy(ref, ref, sem).wait()

    def x_copy(side, c):
        source = obsx.at[c, 1, pl.ds(0, 15)] if side == 0 else obsx.at[c, 2, pl.ds(1, 15)]
        target = obsx.at[c, 3, pl.ds(0, 15)] if side == 0 else obsx.at[c, 0, pl.ds(1, 15)]
        return pltpu.make_async_remote_copy(
            src_ref=source, dst_ref=target, send_sem=sx_s.at[side, c], recv_sem=sx_r.at[side, c],
            device_id=x_sides[side][1], device_id_type=MESH)

    for c in range(CHUNKS):
        for side in range(2):
            @pl.when(x_sides[side][0])
            def _():
                x_copy(side, c).start()

    def send(source, target, send_sem, recv_sem, device):
        pltpu.make_async_remote_copy(
            src_ref=source, dst_ref=target, send_sem=send_sem, recv_sem=recv_sem,
            device_id=device, device_id_type=MESH).start()

    others(lambda d: send(obsx.at[:, pl.ds(1, 2), d], obsb.at[:, :, gz], so_s, so_r, {"gz": d}))
    obsb[:, :, gz] = obsx[:, 1:3, gz]
    for side, first in ((0, 0), (1, 112)):
        parts = [obsx[k // TILES, 1 + j, :, 8 * (k % TILES):8 * (k % TILES) + 8, :].reshape(128, 128)
                 for k in range(4) for j in range(2)]
        obse_s[side] = gather_lanes(parts, 16, first).reshape(16, 8, 128)

        @pl.when(y_sides[side][0])
        def _():
            everyone(lambda d: send(obse_s.at[side, d], obse_r.at[1 - side, gz], se_s.at[2, side, 0],
                                    se_r.at[2, 1 - side, 0], {"gy": y_sides[side][1], "gz": d}))

    store_split(xf, toeplitz(px, 31, 256, 512, 8, 8))
    y_forward(yf, py)
    store_split(zf, toeplitz(pz, 61, 128, 256, 34, 1))
    store_split(za, toeplitz(pz, 61, 128, 256, 94, -1))
    store_split(xa, toeplitz(px, 31, 256, 512, 248, -8))
    y_adjoint(ya, py)
    for part in range(3):
        for ref in (zb, rb):
            ref[part, 0:2] = jnp.zeros((2, 32, 128), F32)
            ref[part, 18:20] = jnp.zeros((2, 32, 128), F32)

    def columns(ref, first, count, c):
        parts = []
        for k in range(TILES):
            groups = [(ref[c, i, :, 8 * k:8 * k + 8, :] if ref.shape[1] < 16 else ref[c, :, i, 8 * k:8 * k + 8, :])
                      .reshape(128, 128) for i in range(first, first + count)]
            parts.append(jnp.concatenate(groups, axis=0))
        return jnp.concatenate(parts, axis=1)

    def tile(value, j):
        return value[:, 128 * j:128 * j + 128]

    def blur_x(matrix, ref, first, c):
        return left_product(matrix, columns(ref, first, 4, c))

    def to_columns(t, value, c):
        parts = [tile(value, k)[128 * j:128 * j + 128] for k in range(TILES) for j in range(2)]
        for k in range(TILES):
            for j in range(2):
                u[t, c, :, j, 8 * k:8 * k + 8, :] = parts[2 * k + j].reshape(16, 8, 128)
        others(lambda d: send(u.at[t, c, d], um.at[t, c, gz], sa_s.at[t, 0], sa_r.at[t, 0, c], {"gz": d}))
        for side, first in ((0, 0), (1, 96)):
            ue_s[t, side, c] = gather_lanes(parts, 32, first).reshape(16, 8, 128)

            @pl.when(y_sides[side][0])
            def _():
                everyone(lambda d: send(ue_s.at[t, side, c, d], ue_r.at[t, 1 - side, c, gz], se_s.at[t, side, c],
                                        se_r.at[t, 1 - side, c], {"gy": y_sides[side][1], "gz": d}))
        um[t, c, gz] = u[t, c, gz]

    def middle(t, own):
        for c in range(CHUNKS):
            z = slice(DEPTH * c, DEPTH * c + DEPTH)
            await_bytes(um.at[t, c, pl.ds(0, 15)], sa_r.at[t, 0, c])
            for side in range(2):
                @pl.when(y_sides[side][0])
                def _():
                    await_bytes(ue_r.at[t, side, c], se_r.at[t, side, c])
            left, right = (ue_r[t, side, c].reshape(128, 128) for side in range(2))
            sides = None
            for j in range(2):
                halo = jnp.concatenate(
                    [spread_lanes(left, right, 32, 2 * k + j).reshape(16, 8, 128) for k in range(TILES)], axis=1)
                own_lanes = um[t, c, :, j].reshape(16 * DEPTH, 128)
                result = right_product(jnp.concatenate([own_lanes, halo.reshape(16 * DEPTH, 128)], axis=1), yf.at[j])
                zb[j, 2:18, z, :] = tile(result, 0).reshape(16, DEPTH, 128)
                sides = tile(result, 1) if sides is None else sides + tile(result, 1)
            zb[2, 2:18, z, :] = sides.reshape(16, DEPTH, 128)
        if t == 0:
            await_bytes(obsb.at[:, :, pl.ds(0, 15)], so_r)
            for side in range(2):
                @pl.when(y_sides[side][0])
                def _():
                    await_bytes(obse_r.at[side], se_r.at[2, side, 0])
            left, right = (obse_r[side].reshape(128, 128) for side in range(2))
            lane = lax.broadcasted_iota(jnp.int32, (128, 128), 1)
            for k in range(4):
                part = spread_lanes(left, right, 32, k)
                obss[:, 8 * k:8 * k + 8, :] = jnp.where(lane < 64, part, 0.0).reshape(16, 8, 128)
        lane = lax.broadcasted_iota(jnp.int32, (128, 128), 1)
        inside = ((lane < 32) & (gy > 0)) | ((lane >= 32) & (lane < 64) & (gy < 3))
        for b in range(4):
            window = jnp.concatenate([zb[j, 4 * b:4 * b + 8].reshape(256, 128) for j in range(3)], axis=1)
            blurred = left_product(zf, window)
            for j in range(2):
                seen = jnp.concatenate([obsb[c, j, 4 * b:4 * b + 4] for c in range(CHUNKS)], axis=1)
                ratio = seen.reshape(128, 128) / tile(blurred, j)
                rb[j, 2 + 4 * b:6 + 4 * b] = ratio.reshape(4, 32, 128)
            ratio = obss[4 * b:4 * b + 4].reshape(128, 128) / jnp.where(inside, tile(blurred, 2), 1.0)
            rb[2, 2 + 4 * b:6 + 4 * b] = jnp.where(inside, ratio, 0.0).reshape(4, 32, 128)
        def far(c, d):
            target = {"gx": 3 - gx, "gz": d}
            if t == 0:
                first = 4 * (gx - 1)

                @pl.when(jnp.logical_not(outer))
                def _():
                    send(wb.at[t, c, d], own.at[c, gz, pl.ds(first, 2)], sf_s.at[t], sf_r.at[t, c], target)

                @pl.when(outer)
                def _():
                    send(wb.at[t, c, d, 2 - gx], own.at[c, gz, first + 2 - gx], sf_s.at[t], sf_r.at[t, c], target)
            else:
                @pl.when(jnp.logical_not(outermost))
                def _():
                    send(wb.at[t, c, d, 2 - gx], own.at[c, gz, 3 * (gx - 1)], sf_s.at[t], sf_r.at[t, c], target)

        def near(c, d):
            send(wb.at[t, c, d], own.at[c, gz, pl.ds(2 - t, 2)], sa_s.at[t, 1], sa_r.at[t, 1, c], {"gz": d})

        for i in range(4):
            b = lax.rem(gz // 4 + 1 + i, 4)
            window = jnp.concatenate([rb[j, pl.ds(4 * b, 8)].reshape(256, 128) for j in range(3)], axis=1)
            back = left_product(za, window)
            for j in range(2):
                result = right_product(jnp.concatenate([tile(back, j), tile(back, 2)], axis=1), ya.at[j])
                result = result.reshape(4, 32, 128)
                for c in range(CHUNKS):
                    wb[t, c, pl.ds(4 * b, 4), j] = result[:, DEPTH * c:DEPTH * c + DEPTH]
            for k in range(4):
                d = 4 * b + lax.rem(gz + 1 + k, 4)

                @pl.when(inner)
                def _():
                    far(0, d)
                if i < 3 or k < 3:
                    near(0, d)
        for c in range(1, CHUNKS):
            @pl.when(inner)
            def _():
                everyone(lambda d: far(c, d))
            others(lambda d: near(c, d))
        own[:, gz, 2 - t:4 - t] = wb[t, :, gz]

    def near_copy(t, ref, c):
        if t == 0:
            source, target = ref.at[c, :, pl.ds(2, 2)], ref.at[c, :, pl.ds(4 * parity, 2)]
        else:
            source, target = ref.at[c, :, 2 - parity], ref.at[c, :, 3 * parity]
        return pltpu.make_async_remote_copy(
            src_ref=source, dst_ref=target, send_sem=sn_s.at[t, c], recv_sem=sn_r.at[t, c],
            device_id={"gx": gx + 1 - 2 * parity}, device_id_type=MESH)

    def arrive_own(t, ref, c):
        await_bytes(ref.at[c, pl.ds(0, 15), pl.ds(2 - t, 2)], sa_r.at[t, 1, c])
        near_copy(t, ref, c).start()

    def arrive_halos(t, ref, c):
        near_copy(t, ref, c).wait_recv()

        @pl.when(inner)
        def _():
            await_bytes(ref.at[c, pl.ds(0, 15), pl.ds(0, 2 - t)], sf_r.at[t, c])

    for c in range(CHUNKS):
        for side in range(2):
            @pl.when(x_sides[side][0])
            def _():
                x_copy(1 - side, c).wait_recv()
        to_columns(0, blur_x(xf, obsx, 0, c), c)
    middle(0, wyx0)

    for c in range(CHUNKS):
        arrive_own(0, wyx0, c)
    for c in range(CHUNKS):
        arrive_halos(0, wyx0, c)
        for half in range(2):
            correction = blur_x(xa, wyx0, 2 * half, c)
            new = columns(obsx, 2 * half, 2, c) * correction
            for k in range(TILES):
                est2[c, 2 * half:2 * half + 2, :, 8 * k:8 * k + 8, :] = tile(new, k).reshape(2, 16, 8, 128)
        to_columns(1, blur_x(xf, est2, 0, c), c)
    middle(1, wyx1)

    for c in range(CHUNKS):
        arrive_own(1, wyx1, c)
    for c in range(CHUNKS):
        arrive_halos(1, wyx1, c)
        correction = blur_x(xa, wyx1, 0, c)
        new_estimate = columns(est2, 1, 2, c) * correction
        for k in range(TILES):
            z = slice(DEPTH * c + 8 * k, DEPTH * c + 8 * k + 8)
            new = tile(new_estimate, k).reshape(32, 8, 128)
            for x in range(32):
                est3[32 * x + z.start:32 * x + z.stop] = new[x]
            for x in range(16):
                pooled_z[32 * x + z.start:32 * x + z.stop] = new[2 * x] + new[2 * x + 1]

    halves = pooled_z[pl.ds(0, 256, stride=2), :] + pooled_z[pl.ds(1, 256, stride=2), :]
    for half in range(2):
        pooled_t[half] = jnp.transpose(halves[128 * half:128 * half + 128])
        even, odd = pooled_t[half, pl.ds(0, 64, stride=2), :], pooled_t[half, pl.ds(1, 64, stride=2), :]
        level = (even + odd) * 0.125
        for d in range(16):
            sent_two[d, 4 * half:4 * half + 4] = level[4 * d:4 * d + 4]
    others(lambda d: send(sent_two.at[d], got_two.at[gz], sp_s, sp_r, {"gz": d}))
    got_two[gz] = sent_two[gz]
    for z in range(32):
        est_ref[32 * z:32 * z + 32] = est3[pl.ds(z, 32, stride=32), :]
    await_bytes(got_two.at[pl.ds(0, 15)], sp_r)
    for c in range(CHUNKS):
        for side in range(2):
            @pl.when(x_sides[side][0])
            def _():
                x_copy(side, c).wait_send()

            @pl.when(y_sides[side][0])
            def _():
                for t in range(2):
                    await_bytes(ue_s.at[t, side, c], se_s.at[t, side, c])
        near_copy(0, wyx0, c).wait_send()
        near_copy(1, wyx1, c).wait_send()
    for side in range(2):
        @pl.when(y_sides[side][0])
        def _():
            await_bytes(obse_s.at[side], se_s.at[2, side, 0])

    @pl.when(inner & jnp.logical_not(outer))
    def _():
        await_bytes(wb.at[0], sf_s.at[0])

    @pl.when(outer)
    def _():
        await_bytes(wb.at[0, :, :, 0], sf_s.at[0])

    @pl.when(inner & jnp.logical_not(outermost))
    def _():
        await_bytes(wb.at[1, :, :, 0], sf_s.at[1])
    for t in range(2):
        for way in range(2):
            await_bytes(wb.at[t, :, pl.ds(0, 15)], sa_s.at[t, way])
    await_bytes(obsb.at[:, :, pl.ds(0, 15)], so_s)
    await_bytes(sent_two.at[pl.ds(0, 15)], sp_s)


def finish(est_in, got_two, est_out, two_out, four_out, eight_out, two_ref, four_ref, eight_ref, part_four, sems):
    copies = [pltpu.make_async_copy(a, b, sems.at[i]) for i, (a, b) in enumerate(
        ((est_in, est_out), (two_ref, two_out), (four_ref, four_out), (eight_ref, eight_out)))]
    copies[0].start()
    group = lax.broadcasted_iota(jnp.int32, (8, 128), 1) // 16
    for half in range(2):
        blocks = [got_two[8 * half + s] for s in range(8)]
        for bit in range(3):
            step = 1 << bit
            upper = (group & step) != 0
            for s in range(8):
                if s & step == 0:
                    a, b = blocks[s], blocks[s + step]
                    blocks[s] = jnp.where(upper, pltpu.roll(b, 16 * step, 1), a)
                    blocks[s + step] = jnp.where(upper, b, pltpu.roll(a, 128 - 16 * step, 1))
        for x in range(8):
            two_ref[x, :, 128 * half:128 * half + 128] = blocks[x][0:4]
            two_ref[8 + x, :, 128 * half:128 * half + 128] = blocks[x][4:8]

    copies[1].start()

    def pool_matrix(rows):
        r = lax.broadcasted_iota(jnp.int32, (rows, rows // 2), 0)
        c = lax.broadcasted_iota(jnp.int32, (rows, rows // 2), 1)
        return jnp.where(r // 2 == c, 0.125, 0.0).astype(F32)

    for a in range(8):
        s = two_ref[2 * a] + two_ref[2 * a + 1]
        part_four[2 * a:2 * a + 1] = s[0:1] + s[1:2]
        part_four[2 * a + 1:2 * a + 2] = s[2:3] + s[3:4]
    four = jnp.dot(part_four[...], pool_matrix(256), precision=lax.Precision.HIGHEST, preferred_element_type=F32)
    for a in range(8):
        four_ref[a] = four[2 * a:2 * a + 2]
    rows = [four[4 * a:4 * a + 1] + four[4 * a + 1:4 * a + 2] + four[4 * a + 2:4 * a + 3] + four[4 * a + 3:4 * a + 4]
            for a in range(4)]
    eight = jnp.dot(jnp.concatenate(rows + rows, axis=0), pool_matrix(128),
                    precision=lax.Precision.HIGHEST, preferred_element_type=F32)
    for a in range(4):
        eight_ref[a] = eight[a:a + 1]

    copies[2].start()
    copies[3].start()
    for copy in copies:
        copy.wait()


def shards(observed, profile_x, profile_y, profile_z):
    vmem = pl.BlockSpec(memory_space=pltpu.VMEM)
    smem = pl.BlockSpec(memory_space=pltpu.SMEM)
    dma = pltpu.SemaphoreType.DMA
    estimate, pieces = pl.pallas_call(
        kernel,
        out_shape=[jax.ShapeDtypeStruct((1024, 128), F32), jax.ShapeDtypeStruct((16, 8, 128), F32)],
        in_specs=[pl.BlockSpec(memory_space=pltpu.HBM), smem, smem, smem],
        out_specs=[vmem] * 2,
        scratch_shapes=[
            pltpu.VMEM((1024, 128), F32),
            dma,
            pltpu.VMEM((2, 256, 512), BF16),
            pltpu.VMEM((2, 256, 512), BF16),
            pltpu.VMEM((2, 2, 256, 256), BF16),
            pltpu.VMEM((2, 2, 256, 128), BF16),
            pltpu.VMEM((2, 128, 256), BF16),
            pltpu.VMEM((2, 128, 256), BF16),
            pltpu.VMEM((CHUNKS, 4, 16, DEPTH, 128), F32),
            pltpu.VMEM((CHUNKS, 2, 16, DEPTH, 128), F32),
            pltpu.VMEM((16, 32, 128), F32),
            pltpu.VMEM((2, 16, 8, 128), F32),
            pltpu.VMEM((2, 16, 8, 128), F32),
            pltpu.VMEM((2, CHUNKS, 16, 2, DEPTH, 128), F32),
            pltpu.VMEM((2, CHUNKS, 16, 2, DEPTH, 128), F32),
            pltpu.VMEM((2, 2, CHUNKS, 16, 8, 128), F32),
            pltpu.VMEM((2, 2, CHUNKS, 16, 8, 128), F32),
            pltpu.VMEM((3, 20, 32, 128), F32),
            pltpu.VMEM((3, 20, 32, 128), F32),
            pltpu.VMEM((2, CHUNKS, 16, 2, DEPTH, 128), F32),
            pltpu.VMEM((CHUNKS, 16, 6, DEPTH, 128), F32),
            pltpu.VMEM((CHUNKS, 16, 4, DEPTH, 128), F32),
            pltpu.VMEM((CHUNKS, 4, 16, DEPTH, 128), F32),
            pltpu.VMEM((1024, 128), F32),
            pltpu.VMEM((512, 128), F32),
            pltpu.VMEM((2, 128, 128), F32),
            pltpu.VMEM((16, 8, 128), F32),
            dma((2, CHUNKS)), dma((2, CHUNKS)),
            dma((2, CHUNKS)), dma((2, CHUNKS)),
            dma((2,)), dma((2, CHUNKS)),
            dma((3, 2, CHUNKS)), dma((3, 2, CHUNKS)),
            dma((2, 2)), dma((2, 2, CHUNKS)),
            dma, dma, dma, dma,
        ],
        compiler_params=pltpu.CompilerParams(
            collective_id=0, has_side_effects=True, vmem_limit_bytes=48 * 1024 * 1024),
        name="deconvolve",
    )(observed.reshape(1024, 128), profile_x, profile_y, profile_z)
    any_space = pl.BlockSpec(memory_space=pl.ANY)
    estimate, two, four, eight = pl.pallas_call(
        finish,
        out_shape=[
            jax.ShapeDtypeStruct((1024, 128), F32),
            jax.ShapeDtypeStruct((16, 4, 256), F32),
            jax.ShapeDtypeStruct((8, 2, 128), F32),
            jax.ShapeDtypeStruct((4, 1, 64), F32),
        ],
        in_specs=[vmem] * 2,
        out_specs=[any_space] * 4,
        scratch_shapes=[
            pltpu.VMEM((16, 4, 256), F32),
            pltpu.VMEM((8, 2, 128), F32),
            pltpu.VMEM((4, 1, 64), F32),
            pltpu.VMEM((16, 256), F32),
            dma((4,)),
        ],
        compiler_params=pltpu.CompilerParams(vmem_limit_bytes=16 * 1024 * 1024),
        name="pyramid",
    )(estimate, pieces)
    return estimate.reshape(32, 32, 128), two, four, eight


def solution(mesh):
    return jax.shard_map(
        shards,
        mesh=mesh,
        in_specs=(P("gz", "gx", "gy"), P(), P(), P()),
        out_specs=(
            P("gz", "gx", "gy"),
            P("gx", ("gy", "gz"), None),
            P("gx", ("gy", "gz"), None),
            P("gx", ("gy", "gz"), None),
        ),
        check_vma=False,
    )
```

```python
import functools

import jax
import jax.numpy as jnp
from jax import lax
from jax.experimental import pallas as pl
from jax.experimental.pallas import tpu as pltpu
from jax.sharding import PartitionSpec as P

MESH = pl.DeviceIdType.MESH
F32, BF16 = jnp.float32, jnp.bfloat16
CHUNKS = 2
DEPTH = 32 // CHUNKS
TILES = DEPTH // 8


SHIFTS = ((0, 0), (2, 2), (1, 2), (2, 1), (2, 3), (3, 2), (0, 2), (1, 1), (1, 3), (2, 0), (3, 1), (3, 3), (0, 1), (0, 3), (1, 0), (3, 0))


def split(value):
    high = value.astype(BF16)
    return high, (value - high.astype(F32)).astype(BF16)


def dot(a, b):
    return jnp.dot(a, b, preferred_element_type=F32)


def left_product(matrix, value):
    high, low = split(value)
    rows = matrix.shape[0] // 2
    both = dot(matrix[...], high)
    return both[0:rows] + (both[rows:] + dot(matrix[0:rows], low))


def right_product(value, matrix):
    high, low = split(value)
    rows = value.shape[0]
    both = dot(jnp.concatenate([high, low], axis=0), matrix[0])
    return both[0:rows] + (both[rows:] + dot(high, matrix[1]))


def toeplitz(taps, count, rows, width, first, step):
    lane = lax.broadcasted_iota(jnp.int32, (8, width), 1)
    base = jnp.zeros((8, width), F32)
    total = taps[0]
    for s in range(count):
        base = jnp.where(lane == first + step * s, taps[s], base)
        if s:
            total = total + taps[s]
    base = base / jnp.full((8, width), total, F32)
    spread = jnp.broadcast_to(base[0:1], (rows, width))
    return pltpu.roll(spread, 0, 1, stride=1, stride_axis=0)


def store_split(ref, value):
    rows = value.shape[0]
    ref[0:rows], ref[rows:] = split(value)


def y_forward(ref, taps):
    full = toeplitz(taps, 31, 256, 256, 255, -1)
    lane = lax.broadcasted_iota(jnp.int32, (256, 128), 1) // 16
    own = pltpu.roll(full, 240, 1)[:, 0:128]
    for j in range(2):
        left = pltpu.roll(full, 16 * j, 1)[:, 0:128] if j else full[:, 0:128]
        right = pltpu.roll(full, 144 + 16 * j, 1)[:, 0:128]
        side = jnp.where(lane == j, left, jnp.where(lane == 2 + j, right, 0.0))
        for i, part in enumerate(split(jnp.concatenate([own, side], axis=1))):
            ref[j, i, 0:128] = part[32:160]
            ref[j, i, 128:160] = part[0:32]
            ref[j, i, 160:192] = part[160:192]
            ref[j, i, 192:256] = jnp.zeros((64, 256), BF16)


def y_adjoint(ref, taps):
    full = toeplitz(taps, 31, 256, 256, 225, 1)[:, 0:128]
    for i, part in enumerate(split(full)):
        for j in range(2):
            ref[j, i, 128:256] = jnp.zeros((128, 128), BF16)
            ref[j, i, 0:128] = part[16:144]
            ref[j, i, 128 + 16 * j:144 + 16 * j] = part[0:16]
            ref[j, i, 160 + 16 * j:176 + 16 * j] = part[144:160]


def gather_lanes(parts, width, first):
    lane = lax.broadcasted_iota(jnp.int32, parts[0].shape, 1) // width
    result = None
    for k, part in enumerate(parts):
        shift = (width * k - first) % 128
        moved = pltpu.roll(part, shift, 1) if shift else part
        result = moved if result is None else jnp.where(lane == k, moved, result)
    return result


def spread_lanes(left, right, width, k):
    lane = lax.broadcasted_iota(jnp.int32, left.shape, 1)
    a, b = (128 - width * k) % 128, (width - width * k) % 128
    left = pltpu.roll(left, a, 1) if a else left
    right = pltpu.roll(right, b, 1) if b else right
    return jnp.where(lane < width, left, right)


def kernel(obs_hbm, px, py, pz, est_ref, got_two,
           obs_ref, obs_sem, xf, xa, yf, ya, zf, za, obsx, obsb, obss, obse_s, obse_r, u, um, ue_s, ue_r, zb, ratios, rb, wb,
           wyx0, wyx1, est2, est3, pooled_z, pooled_t, sent_two,
           sx_s, sx_r, sn_s, sn_r, sf_s, sf_r, se_s, se_r, sa_s, sa_r, so_s, so_r, sp_s, sp_r):
    gx, gy, gz = lax.axis_index("gx"), lax.axis_index("gy"), lax.axis_index("gz")
    x_sides = ((gx > 0, {"gx": gx - 1}), (gx < 3, {"gx": gx + 1}))
    y_sides = ((gy > 0, gy - 1), (gy < 3, gy + 1))
    inner = (gx == 1) | (gx == 2)
    outermost = ((gx == 1) & (gz == 0)) | ((gx == 2) & (gz == 15))
    outer = ((gx == 1) & (gz < 2)) | ((gx == 2) & (gz > 13))
    parity = lax.rem(gx, 2)

    load = pltpu.make_async_copy(obs_hbm, obs_ref, obs_sem)
    load.start()

    obsx[:, 0, 0] = jnp.zeros((CHUNKS, DEPTH, 128), F32)
    obsx[:, 3, 15] = jnp.zeros((CHUNKS, DEPTH, 128), F32)
    wyx0[:, 0:2, 0] = jnp.zeros((CHUNKS, 2, DEPTH, 128), F32)
    wyx0[:, 14:16, 5] = jnp.zeros((CHUNKS, 2, DEPTH, 128), F32)
    wyx1[:, 0, 0] = jnp.zeros((CHUNKS, DEPTH, 128), F32)
    wyx1[:, 15, 3] = jnp.zeros((CHUNKS, DEPTH, 128), F32)

    @pl.when(gx == 0)
    def _():
        obsx[:, 0] = jnp.zeros((CHUNKS, 16, DEPTH, 128), F32)
        wyx0[:, :, 0:2] = jnp.zeros((CHUNKS, 16, 2, DEPTH, 128), F32)
        wyx1[:, :, 0] = jnp.zeros((CHUNKS, 16, DEPTH, 128), F32)

    @pl.when(gx == 3)
    def _():
        obsx[:, 3] = jnp.zeros((CHUNKS, 16, DEPTH, 128), F32)
        wyx0[:, :, 4:6] = jnp.zeros((CHUNKS, 16, 2, DEPTH, 128), F32)
        wyx1[:, :, 3] = jnp.zeros((CHUNKS, 16, DEPTH, 128), F32)

    for side in range(2):
        @pl.when(jnp.logical_not(y_sides[side][0]))
        def _():
            obse_r[side] = jnp.zeros((16, 8, 128), F32)
            for t in range(2):
                ue_r[t, side] = jnp.zeros((CHUNKS, 16, 8, 128), F32)

    barrier = pltpu.get_barrier_semaphore()

    def greet(target):
        pl.semaphore_signal(barrier, inc=1, device_id=target, device_id_type=MESH)

    def shifted(k, first):
        a, b = SHIFTS[k + first]
        return 4 * lax.rem(gz // 4 + a, 4) + lax.rem(gz + b, 4)

    def others(body):
        for k in range(15):
            body(shifted(k, 1))

    def everyone(body):
        for k in range(16):
            body(shifted(k, 0))

    greet({"gx": gx + 1 - 2 * parity})

    @pl.when(inner)
    def _():
        everyone(lambda d: greet({"gx": 3 - gx, "gz": d}))
    others(lambda d: greet({"gz": d}))
    for there, target in y_sides:
        @pl.when(there)
        def _():
            everyone(lambda d: greet({"gy": target, "gz": d}))

    load.wait()
    for x in range(32):
        row = obs_ref[pl.ds(x, 32, stride=32), :]
        for c in range(CHUNKS):
            obsx[c, 1 + x // 16, x % 16] = row[DEPTH * c:DEPTH * c + DEPTH]

    neighbours = sum(there.astype(jnp.int32) for there, _ in y_sides) + inner.astype(jnp.int32)
    pl.semaphore_wait(barrier, 16 + 16 * neighbours)

    def await_bytes(ref, sem):
        pltpu.make_async_copy(ref, ref, sem).wait()

    def x_copy(side, c):
        source = obsx.at[c, 1, pl.ds(0, 15)] if side == 0 else obsx.at[c, 2, pl.ds(1, 15)]
        target = obsx.at[c, 3, pl.ds(0, 15)] if side == 0 else obsx.at[c, 0, pl.ds(1, 15)]
        return pltpu.make_async_remote_copy(
            src_ref=source, dst_ref=target, send_sem=sx_s.at[side, c], recv_sem=sx_r.at[side, c],
            device_id=x_sides[side][1], device_id_type=MESH)

    for c in range(CHUNKS):
        for side in range(2):
            @pl.when(x_sides[side][0])
            def _():
                x_copy(side, c).start()

    def send(source, target, send_sem, recv_sem, device):
        pltpu.make_async_remote_copy(
            src_ref=source, dst_ref=target, send_sem=send_sem, recv_sem=recv_sem,
            device_id=device, device_id_type=MESH).start()

    others(lambda d: send(obsx.at[:, pl.ds(1, 2), d], obsb.at[:, :, gz], so_s, so_r, {"gz": d}))
    obsb[:, :, gz] = obsx[:, 1:3, gz]
    for side, first in ((0, 0), (1, 112)):
        parts = [obsx[k // TILES, 1 + j, :, 8 * (k % TILES):8 * (k % TILES) + 8, :].reshape(128, 128)
                 for k in range(4) for j in range(2)]
        obse_s[side] = gather_lanes(parts, 16, first).reshape(16, 8, 128)

        @pl.when(y_sides[side][0])
        def _():
            everyone(lambda d: send(obse_s.at[side, d], obse_r.at[1 - side, gz], se_s.at[2, side, 0],
                                    se_r.at[2, 1 - side, 0], {"gy": y_sides[side][1], "gz": d}))

    store_split(xf, toeplitz(px, 31, 256, 512, 8, 8))
    y_forward(yf, py)
    store_split(zf, toeplitz(pz, 61, 128, 256, 34, 1))
    store_split(za, toeplitz(pz, 61, 128, 256, 94, -1))
    store_split(xa, toeplitz(px, 31, 256, 512, 248, -8))
    y_adjoint(ya, py)
    for ref, parts in ((zb, 3), (rb, 2)):
        for part in range(parts):
            ref[part, 0:2] = jnp.zeros((2, 32, 128), F32)
            ref[part, 18:20] = jnp.zeros((2, 32, 128), F32)

    def columns(ref, first, count, c):
        parts = []
        for k in range(TILES):
            groups = [(ref[c, i, :, 8 * k:8 * k + 8, :] if ref.shape[1] < 16 else ref[c, :, i, 8 * k:8 * k + 8, :])
                      .reshape(128, 128) for i in range(first, first + count)]
            parts.append(jnp.concatenate(groups, axis=0))
        return jnp.concatenate(parts, axis=1)

    def tile(value, j):
        return value[:, 128 * j:128 * j + 128]

    def blur_x(matrix, ref, first, c):
        return left_product(matrix, columns(ref, first, 4, c))

    def to_columns(t, value, c):
        parts = [tile(value, k)[128 * j:128 * j + 128] for k in range(TILES) for j in range(2)]
        for k in range(TILES):
            for j in range(2):
                u[t, c, :, j, 8 * k:8 * k + 8, :] = parts[2 * k + j].reshape(16, 8, 128)
        others(lambda d: send(u.at[t, c, d], um.at[t, c, gz], sa_s.at[t, 0], sa_r.at[t, 0, c], {"gz": d}))
        for side, first in ((0, 0), (1, 96)):
            ue_s[t, side, c] = gather_lanes(parts, 32, first).reshape(16, 8, 128)

            @pl.when(y_sides[side][0])
            def _():
                everyone(lambda d: send(ue_s.at[t, side, c, d], ue_r.at[t, 1 - side, c, gz], se_s.at[t, side, c],
                                        se_r.at[t, 1 - side, c], {"gy": y_sides[side][1], "gz": d}))
        um[t, c, gz] = u[t, c, gz]

    def middle(t, own):
        for c in range(CHUNKS):
            z = slice(DEPTH * c, DEPTH * c + DEPTH)
            await_bytes(um.at[t, c, pl.ds(0, 15)], sa_r.at[t, 0, c])
            for side in range(2):
                @pl.when(y_sides[side][0])
                def _():
                    await_bytes(ue_r.at[t, side, c], se_r.at[t, side, c])
            left, right = (ue_r[t, side, c].reshape(128, 128) for side in range(2))
            sides = None
            for j in range(2):
                halo = jnp.concatenate(
                    [spread_lanes(left, right, 32, 2 * k + j).reshape(16, 8, 128) for k in range(TILES)], axis=1)
                own_lanes = um[t, c, :, j].reshape(16 * DEPTH, 128)
                result = right_product(jnp.concatenate([own_lanes, halo.reshape(16 * DEPTH, 128)], axis=1), yf.at[j])
                zb[j, 2:18, z, :] = tile(result, 0).reshape(16, DEPTH, 128)
                sides = tile(result, 1) if sides is None else sides + tile(result, 1)
            zb[2, 2:18, z, :] = sides.reshape(16, DEPTH, 128)
        if t == 0:
            await_bytes(obsb.at[:, :, pl.ds(0, 15)], so_r)
            for side in range(2):
                @pl.when(y_sides[side][0])
                def _():
                    await_bytes(obse_r.at[side], se_r.at[2, side, 0])
            left, right = (obse_r[side].reshape(128, 128) for side in range(2))
            lane = lax.broadcasted_iota(jnp.int32, (128, 128), 1)
            for k in range(4):
                part = spread_lanes(left, right, 32, k)
                obss[:, 8 * k:8 * k + 8, :] = jnp.where(lane < 64, part, 0.0).reshape(16, 8, 128)
        lane = lax.broadcasted_iota(jnp.int32, (128, 128), 1)
        inside = ((lane < 32) & (gy > 0)) | ((lane >= 32) & (lane < 64) & (gy < 3))
        for b in range(4):
            window = jnp.concatenate([zb[j, 4 * b:4 * b + 8].reshape(256, 128) for j in range(3)], axis=1)
            blurred = left_product(zf, window)
            for j in range(2):
                seen = jnp.concatenate([obsb[c, j, 4 * b:4 * b + 4] for c in range(CHUNKS)], axis=1)
                ratios[j, 128 * b:128 * b + 128] = seen.reshape(128, 128) / tile(blurred, j)
            ratio = obss[4 * b:4 * b + 4].reshape(128, 128) / jnp.where(inside, tile(blurred, 2), 1.0)
            ratios[2, 128 * b:128 * b + 128] = jnp.where(inside, ratio, 0.0)
        for j in range(2):
            result = right_product(jnp.concatenate([ratios[j], ratios[2]], axis=1), ya.at[j])
            rb[j, 2:18] = result.reshape(16, 32, 128)

        def far(c, d):
            target = {"gx": 3 - gx, "gz": d}
            if t == 0:
                first = 4 * (gx - 1)

                @pl.when(jnp.logical_not(outer))
                def _():
                    send(wb.at[t, c, d], own.at[c, gz, pl.ds(first, 2)], sf_s.at[t], sf_r.at[t, c], target)

                @pl.when(outer)
                def _():
                    send(wb.at[t, c, d, 2 - gx], own.at[c, gz, first + 2 - gx], sf_s.at[t], sf_r.at[t, c], target)
            else:
                @pl.when(jnp.logical_not(outermost))
                def _():
                    send(wb.at[t, c, d, 2 - gx], own.at[c, gz, 3 * (gx - 1)], sf_s.at[t], sf_r.at[t, c], target)

        def near(c, d):
            send(wb.at[t, c, d], own.at[c, gz, pl.ds(2 - t, 2)], sa_s.at[t, 1], sa_r.at[t, 1, c], {"gz": d})

        for i in range(4):
            b = lax.rem(gz // 4 + (2, 1, 3, 0)[i], 4)
            window = jnp.concatenate([rb[j, pl.ds(4 * b, 8)].reshape(256, 128) for j in range(2)], axis=1)
            back = left_product(za, window)
            for j in range(2):
                result = tile(back, j).reshape(4, 32, 128)
                for c in range(CHUNKS):
                    wb[t, c, pl.ds(4 * b, 4), j] = result[:, DEPTH * c:DEPTH * c + DEPTH]
            for k in range(4):
                d = 4 * b + lax.rem(gz + (2, 1, 3, 0)[k], 4)

                @pl.when(inner)
                def _():
                    far(0, d)
                if i < 3 or k < 3:
                    near(0, d)
        for c in range(1, CHUNKS):
            others(lambda d: near(c, d))

            @pl.when(inner)
            def _():
                everyone(lambda d: far(c, d))
        own[:, gz, 2 - t:4 - t] = wb[t, :, gz]

    def near_copy(t, ref, c):
        if t == 0:
            source, target = ref.at[c, :, pl.ds(2, 2)], ref.at[c, :, pl.ds(4 * parity, 2)]
        else:
            source, target = ref.at[c, :, 2 - parity], ref.at[c, :, 3 * parity]
        return pltpu.make_async_remote_copy(
            src_ref=source, dst_ref=target, send_sem=sn_s.at[t, c], recv_sem=sn_r.at[t, c],
            device_id={"gx": gx + 1 - 2 * parity}, device_id_type=MESH)

    def arrive_own(t, ref, c):
        await_bytes(ref.at[c, pl.ds(0, 15), pl.ds(2 - t, 2)], sa_r.at[t, 1, c])
        near_copy(t, ref, c).start()

    def arrive_halos(t, ref, c):
        near_copy(t, ref, c).wait_recv()

        @pl.when(inner)
        def _():
            await_bytes(ref.at[c, pl.ds(0, 15), pl.ds(0, 2 - t)], sf_r.at[t, c])

    for c in range(CHUNKS):
        for side in range(2):
            @pl.when(x_sides[side][0])
            def _():
                x_copy(1 - side, c).wait_recv()
        to_columns(0, blur_x(xf, obsx, 0, c), c)
    middle(0, wyx0)

    for c in range(CHUNKS):
        arrive_own(0, wyx0, c)
    for c in range(CHUNKS):
        arrive_halos(0, wyx0, c)
        for half in range(2):
            correction = blur_x(xa, wyx0, 2 * half, c)
            new = columns(obsx, 2 * half, 2, c) * correction
            for k in range(TILES):
                est2[c, 2 * half:2 * half + 2, :, 8 * k:8 * k + 8, :] = tile(new, k).reshape(2, 16, 8, 128)
        to_columns(1, blur_x(xf, est2, 0, c), c)
    middle(1, wyx1)

    for c in range(CHUNKS):
        arrive_own(1, wyx1, c)
    for c in range(CHUNKS):
        arrive_halos(1, wyx1, c)
        correction = blur_x(xa, wyx1, 0, c)
        new_estimate = columns(est2, 1, 2, c) * correction
        for k in range(TILES):
            z = slice(DEPTH * c + 8 * k, DEPTH * c + 8 * k + 8)
            new = tile(new_estimate, k).reshape(32, 8, 128)
            for x in range(32):
                est3[32 * x + z.start:32 * x + z.stop] = new[x]
            for x in range(16):
                pooled_z[32 * x + z.start:32 * x + z.stop] = new[2 * x] + new[2 * x + 1]

    halves = pooled_z[pl.ds(0, 256, stride=2), :] + pooled_z[pl.ds(1, 256, stride=2), :]
    for half in range(2):
        pooled_t[half] = jnp.transpose(halves[128 * half:128 * half + 128])
        even, odd = pooled_t[half, pl.ds(0, 64, stride=2), :], pooled_t[half, pl.ds(1, 64, stride=2), :]
        level = (even + odd) * 0.125
        for d in range(16):
            sent_two[d, 4 * half:4 * half + 4] = level[4 * d:4 * d + 4]
    others(lambda d: send(sent_two.at[d], got_two.at[gz], sp_s, sp_r, {"gz": d}))
    got_two[gz] = sent_two[gz]
    for z in range(32):
        est_ref[32 * z:32 * z + 32] = est3[pl.ds(z, 32, stride=32), :]
    await_bytes(got_two.at[pl.ds(0, 15)], sp_r)
    for c in range(CHUNKS):
        for side in range(2):
            @pl.when(x_sides[side][0])
            def _():
                x_copy(side, c).wait_send()

            @pl.when(y_sides[side][0])
            def _():
                for t in range(2):
                    await_bytes(ue_s.at[t, side, c], se_s.at[t, side, c])
        near_copy(0, wyx0, c).wait_send()
        near_copy(1, wyx1, c).wait_send()
    for side in range(2):
        @pl.when(y_sides[side][0])
        def _():
            await_bytes(obse_s.at[side], se_s.at[2, side, 0])

    @pl.when(inner & jnp.logical_not(outer))
    def _():
        await_bytes(wb.at[0], sf_s.at[0])

    @pl.when(outer)
    def _():
        await_bytes(wb.at[0, :, :, 0], sf_s.at[0])

    @pl.when(inner & jnp.logical_not(outermost))
    def _():
        await_bytes(wb.at[1, :, :, 0], sf_s.at[1])
    for t in range(2):
        for way in range(2):
            await_bytes(wb.at[t, :, pl.ds(0, 15)], sa_s.at[t, way])
    await_bytes(obsb.at[:, :, pl.ds(0, 15)], so_s)
    await_bytes(sent_two.at[pl.ds(0, 15)], sp_s)


def finish(est_in, got_two, est_out, two_out, four_out, eight_out, two_ref, four_ref, eight_ref, part_four, sems):
    copies = [pltpu.make_async_copy(a, b, sems.at[i]) for i, (a, b) in enumerate(
        ((est_in, est_out), (two_ref, two_out), (four_ref, four_out), (eight_ref, eight_out)))]
    copies[0].start()
    group = lax.broadcasted_iota(jnp.int32, (8, 128), 1) // 16
    for half in range(2):
        blocks = [got_two[8 * half + s] for s in range(8)]
        for bit in range(3):
            step = 1 << bit
            upper = (group & step) != 0
            for s in range(8):
                if s & step == 0:
                    a, b = blocks[s], blocks[s + step]
                    blocks[s] = jnp.where(upper, pltpu.roll(b, 16 * step, 1), a)
                    blocks[s + step] = jnp.where(upper, b, pltpu.roll(a, 128 - 16 * step, 1))
        for x in range(8):
            two_ref[x, :, 128 * half:128 * half + 128] = blocks[x][0:4]
            two_ref[8 + x, :, 128 * half:128 * half + 128] = blocks[x][4:8]

    copies[1].start()

    def pool_matrix(rows):
        r = lax.broadcasted_iota(jnp.int32, (rows, rows // 2), 0)
        c = lax.broadcasted_iota(jnp.int32, (rows, rows // 2), 1)
        return jnp.where(r // 2 == c, 0.125, 0.0).astype(F32)

    for a in range(8):
        s = two_ref[2 * a] + two_ref[2 * a + 1]
        part_four[2 * a:2 * a + 1] = s[0:1] + s[1:2]
        part_four[2 * a + 1:2 * a + 2] = s[2:3] + s[3:4]
    four = jnp.dot(part_four[...], pool_matrix(256), precision=lax.Precision.HIGHEST, preferred_element_type=F32)
    for a in range(8):
        four_ref[a] = four[2 * a:2 * a + 2]
    rows = [four[4 * a:4 * a + 1] + four[4 * a + 1:4 * a + 2] + four[4 * a + 2:4 * a + 3] + four[4 * a + 3:4 * a + 4]
            for a in range(4)]
    eight = jnp.dot(jnp.concatenate(rows + rows, axis=0), pool_matrix(128),
                    precision=lax.Precision.HIGHEST, preferred_element_type=F32)
    for a in range(4):
        eight_ref[a] = eight[a:a + 1]

    copies[2].start()
    copies[3].start()
    for copy in copies:
        copy.wait()


def shards(observed, profile_x, profile_y, profile_z):
    vmem = pl.BlockSpec(memory_space=pltpu.VMEM)
    smem = pl.BlockSpec(memory_space=pltpu.SMEM)
    dma = pltpu.SemaphoreType.DMA
    estimate, pieces = pl.pallas_call(
        kernel,
        out_shape=[jax.ShapeDtypeStruct((1024, 128), F32), jax.ShapeDtypeStruct((16, 8, 128), F32)],
        in_specs=[pl.BlockSpec(memory_space=pltpu.HBM), smem, smem, smem],
        out_specs=[vmem] * 2,
        scratch_shapes=[
            pltpu.VMEM((1024, 128), F32),
            dma,
            pltpu.VMEM((512, 512), BF16),
            pltpu.VMEM((512, 512), BF16),
            pltpu.VMEM((2, 2, 256, 256), BF16),
            pltpu.VMEM((2, 2, 256, 128), BF16),
            pltpu.VMEM((256, 256), BF16),
            pltpu.VMEM((256, 256), BF16),
            pltpu.VMEM((CHUNKS, 4, 16, DEPTH, 128), F32),
            pltpu.VMEM((CHUNKS, 2, 16, DEPTH, 128), F32),
            pltpu.VMEM((16, 32, 128), F32),
            pltpu.VMEM((2, 16, 8, 128), F32),
            pltpu.VMEM((2, 16, 8, 128), F32),
            pltpu.VMEM((2, CHUNKS, 16, 2, DEPTH, 128), F32),
            pltpu.VMEM((2, CHUNKS, 16, 2, DEPTH, 128), F32),
            pltpu.VMEM((2, 2, CHUNKS, 16, 8, 128), F32),
            pltpu.VMEM((2, 2, CHUNKS, 16, 8, 128), F32),
            pltpu.VMEM((3, 20, 32, 128), F32),
            pltpu.VMEM((3, 512, 128), F32),
            pltpu.VMEM((2, 20, 32, 128), F32),
            pltpu.VMEM((2, CHUNKS, 16, 2, DEPTH, 128), F32),
            pltpu.VMEM((CHUNKS, 16, 6, DEPTH, 128), F32),
            pltpu.VMEM((CHUNKS, 16, 4, DEPTH, 128), F32),
            pltpu.VMEM((CHUNKS, 4, 16, DEPTH, 128), F32),
            pltpu.VMEM((1024, 128), F32),
            pltpu.VMEM((512, 128), F32),
            pltpu.VMEM((2, 128, 128), F32),
            pltpu.VMEM((16, 8, 128), F32),
            dma((2, CHUNKS)), dma((2, CHUNKS)),
            dma((2, CHUNKS)), dma((2, CHUNKS)),
            dma((2,)), dma((2, CHUNKS)),
            dma((3, 2, CHUNKS)), dma((3, 2, CHUNKS)),
            dma((2, 2)), dma((2, 2, CHUNKS)),
            dma, dma, dma, dma,
        ],
        compiler_params=pltpu.CompilerParams(
            collective_id=0, has_side_effects=True, vmem_limit_bytes=48 * 1024 * 1024),
        name="deconvolve",
    )(observed.reshape(1024, 128), profile_x, profile_y, profile_z)
    any_space = pl.BlockSpec(memory_space=pl.ANY)
    estimate, two, four, eight = pl.pallas_call(
        finish,
        out_shape=[
            jax.ShapeDtypeStruct((1024, 128), F32),
            jax.ShapeDtypeStruct((16, 4, 256), F32),
            jax.ShapeDtypeStruct((8, 2, 128), F32),
            jax.ShapeDtypeStruct((4, 1, 64), F32),
        ],
        in_specs=[vmem] * 2,
        out_specs=[any_space] * 4,
        scratch_shapes=[
            pltpu.VMEM((16, 4, 256), F32),
            pltpu.VMEM((8, 2, 128), F32),
            pltpu.VMEM((4, 1, 64), F32),
            pltpu.VMEM((16, 256), F32),
            dma((4,)),
        ],
        compiler_params=pltpu.CompilerParams(vmem_limit_bytes=16 * 1024 * 1024),
        name="pyramid",
    )(estimate, pieces)
    return estimate.reshape(32, 32, 128), two, four, eight


def solution(mesh):
    return jax.shard_map(
        shards,
        mesh=mesh,
        in_specs=(P("gz", "gx", "gy"), P(), P(), P()),
        out_specs=(
            P("gz", "gx", "gy"),
            P("gx", ("gy", "gz"), None),
            P("gx", ("gy", "gz"), None),
            P("gx", ("gy", "gz"), None),
        ),
        check_vma=False,
    )
```

```python
import functools

import jax
import jax.numpy as jnp
from jax import lax
from jax.experimental import pallas as pl
from jax.experimental.pallas import tpu as pltpu
from jax.sharding import PartitionSpec as P

MESH = pl.DeviceIdType.MESH
F32, BF16 = jnp.float32, jnp.bfloat16
CHUNKS = 2
DEPTH = 32 // CHUNKS
TILES = DEPTH // 8


SHIFTS = ((0, 0), (2, 2), (2, 1), (2, 3), (2, 0), (1, 2), (3, 2), (1, 1), (1, 3), (3, 1), (3, 3), (1, 0), (3, 0), (0, 2), (0, 1), (0, 3))


def split(value):
    high = value.astype(BF16)
    return high, (value - high.astype(F32)).astype(BF16)


def dot(a, b):
    return jnp.dot(a, b, preferred_element_type=F32)


def left_product(matrix, value):
    high, low = split(value)
    rows = matrix.shape[0] // 2
    both = dot(matrix[...], high)
    return both[0:rows] + (both[rows:] + dot(matrix[0:rows], low))


def right_product(value, matrix):
    high, low = split(value)
    rows = value.shape[0]
    both = dot(jnp.concatenate([high, low], axis=0), matrix[0])
    return both[0:rows] + (both[rows:] + dot(high, matrix[1]))


def toeplitz(taps, count, rows, width, first, step):
    lane = lax.broadcasted_iota(jnp.int32, (8, width), 1)
    base = jnp.zeros((8, width), F32)
    total = taps[0]
    for s in range(count):
        base = jnp.where(lane == first + step * s, taps[s], base)
        if s:
            total = total + taps[s]
    base = base / jnp.full((8, width), total, F32)
    spread = jnp.broadcast_to(base[0:1], (rows, width))
    return pltpu.roll(spread, 0, 1, stride=1, stride_axis=0)


def store_split(ref, value):
    rows = value.shape[0]
    ref[0:rows], ref[rows:] = split(value)


def y_forward(ref, taps):
    full = toeplitz(taps, 31, 256, 256, 255, -1)
    lane = lax.broadcasted_iota(jnp.int32, (256, 128), 1) // 16
    own = pltpu.roll(full, 240, 1)[:, 0:128]
    for j in range(2):
        left = pltpu.roll(full, 16 * j, 1)[:, 0:128] if j else full[:, 0:128]
        right = pltpu.roll(full, 144 + 16 * j, 1)[:, 0:128]
        side = jnp.where(lane == j, left, jnp.where(lane == 2 + j, right, 0.0))
        for i, part in enumerate(split(jnp.concatenate([own, side], axis=1))):
            ref[j, i, 0:128] = part[32:160]
            ref[j, i, 128:160] = part[0:32]
            ref[j, i, 160:192] = part[160:192]
            ref[j, i, 192:256] = jnp.zeros((64, 256), BF16)


def y_adjoint(ref, taps):
    full = toeplitz(taps, 31, 256, 256, 225, 1)[:, 0:128]
    for i, part in enumerate(split(full)):
        for j in range(2):
            ref[j, i, 128:256] = jnp.zeros((128, 128), BF16)
            ref[j, i, 0:128] = part[16:144]
            ref[j, i, 128 + 16 * j:144 + 16 * j] = part[0:16]
            ref[j, i, 160 + 16 * j:176 + 16 * j] = part[144:160]


def gather_lanes(parts, width, first):
    lane = lax.broadcasted_iota(jnp.int32, parts[0].shape, 1) // width
    result = None
    for k, part in enumerate(parts):
        shift = (width * k - first) % 128
        moved = pltpu.roll(part, shift, 1) if shift else part
        result = moved if result is None else jnp.where(lane == k, moved, result)
    return result


def spread_lanes(left, right, width, k):
    lane = lax.broadcasted_iota(jnp.int32, left.shape, 1)
    a, b = (128 - width * k) % 128, (width - width * k) % 128
    left = pltpu.roll(left, a, 1) if a else left
    right = pltpu.roll(right, b, 1) if b else right
    return jnp.where(lane < width, left, right)


def kernel(obs_hbm, px, py, pz, est_ref, got_two,
           obs_ref, obs_sem, xf, xa, yf, ya, zf, za, obsx, obsb, obss, obse_s, obse_r, u, um, ue_s, ue_r, zb, ratios, rb, wb,
           wyx0, wyx1, est2, est3, pooled_z, pooled_t, sent_two,
           sx_s, sx_r, sn_s, sn_r, sf_s, sf_r, se_s, se_r, sa_s, sa_r, so_s, so_r, sp_s, sp_r):
    gx, gy, gz = lax.axis_index("gx"), lax.axis_index("gy"), lax.axis_index("gz")
    x_sides = ((gx > 0, {"gx": gx - 1}), (gx < 3, {"gx": gx + 1}))
    y_sides = ((gy > 0, gy - 1), (gy < 3, gy + 1))
    inner = (gx == 1) | (gx == 2)
    outermost = ((gx == 1) & (gz == 0)) | ((gx == 2) & (gz == 15))
    outer = ((gx == 1) & (gz < 2)) | ((gx == 2) & (gz > 13))
    parity = lax.rem(gx, 2)

    load = pltpu.make_async_copy(obs_hbm, obs_ref, obs_sem)
    load.start()

    obsx[:, 0, 0] = jnp.zeros((CHUNKS, DEPTH, 128), F32)
    obsx[:, 3, 15] = jnp.zeros((CHUNKS, DEPTH, 128), F32)
    wyx0[:, 0:2, 0] = jnp.zeros((CHUNKS, 2, DEPTH, 128), F32)
    wyx0[:, 14:16, 5] = jnp.zeros((CHUNKS, 2, DEPTH, 128), F32)
    wyx1[:, 0, 0] = jnp.zeros((CHUNKS, DEPTH, 128), F32)
    wyx1[:, 15, 3] = jnp.zeros((CHUNKS, DEPTH, 128), F32)

    @pl.when(gx == 0)
    def _():
        obsx[:, 0] = jnp.zeros((CHUNKS, 16, DEPTH, 128), F32)
        wyx0[:, :, 0:2] = jnp.zeros((CHUNKS, 16, 2, DEPTH, 128), F32)
        wyx1[:, :, 0] = jnp.zeros((CHUNKS, 16, DEPTH, 128), F32)

    @pl.when(gx == 3)
    def _():
        obsx[:, 3] = jnp.zeros((CHUNKS, 16, DEPTH, 128), F32)
        wyx0[:, :, 4:6] = jnp.zeros((CHUNKS, 16, 2, DEPTH, 128), F32)
        wyx1[:, :, 3] = jnp.zeros((CHUNKS, 16, DEPTH, 128), F32)

    for side in range(2):
        @pl.when(jnp.logical_not(y_sides[side][0]))
        def _():
            obse_r[side] = jnp.zeros((16, 8, 128), F32)
            for t in range(2):
                ue_r[t, side] = jnp.zeros((CHUNKS, 16, 8, 128), F32)

    barrier = pltpu.get_barrier_semaphore()

    def greet(target):
        pl.semaphore_signal(barrier, inc=1, device_id=target, device_id_type=MESH)

    def shifted(k, first):
        a, b = SHIFTS[k + first]
        return 4 * lax.rem(gz // 4 + a, 4) + lax.rem(gz + b, 4)

    def others(body):
        for k in range(15):
            body(shifted(k, 1))

    def everyone(body):
        for k in range(16):
            body(shifted((k + 1) % 16, 0))

    greet({"gx": gx + 1 - 2 * parity})

    @pl.when(inner)
    def _():
        everyone(lambda d: greet({"gx": 3 - gx, "gz": d}))
    others(lambda d: greet({"gz": d}))
    for there, target in y_sides:
        @pl.when(there)
        def _():
            everyone(lambda d: greet({"gy": target, "gz": d}))

    load.wait()
    for x in range(32):
        row = obs_ref[pl.ds(x, 32, stride=32), :]
        for c in range(CHUNKS):
            obsx[c, 1 + x // 16, x % 16] = row[DEPTH * c:DEPTH * c + DEPTH]

    neighbours = sum(there.astype(jnp.int32) for there, _ in y_sides) + inner.astype(jnp.int32)
    pl.semaphore_wait(barrier, 16 + 16 * neighbours)

    def await_bytes(ref, sem):
        pltpu.make_async_copy(ref, ref, sem).wait()

    def x_copy(side, c):
        source = obsx.at[c, 1, pl.ds(0, 15)] if side == 0 else obsx.at[c, 2, pl.ds(1, 15)]
        target = obsx.at[c, 3, pl.ds(0, 15)] if side == 0 else obsx.at[c, 0, pl.ds(1, 15)]
        return pltpu.make_async_remote_copy(
            src_ref=source, dst_ref=target, send_sem=sx_s.at[side, c], recv_sem=sx_r.at[side, c],
            device_id=x_sides[side][1], device_id_type=MESH)

    for c in range(CHUNKS):
        for side in range(2):
            @pl.when(x_sides[side][0])
            def _():
                x_copy(side, c).start()

    def send(source, target, send_sem, recv_sem, device):
        pltpu.make_async_remote_copy(
            src_ref=source, dst_ref=target, send_sem=send_sem, recv_sem=recv_sem,
            device_id=device, device_id_type=MESH).start()

    others(lambda d: send(obsx.at[:, pl.ds(1, 2), d], obsb.at[:, :, gz], so_s, so_r, {"gz": d}))
    obsb[:, :, gz] = obsx[:, 1:3, gz]
    for side, first in ((0, 0), (1, 112)):
        parts = [obsx[k // TILES, 1 + j, :, 8 * (k % TILES):8 * (k % TILES) + 8, :].reshape(128, 128)
                 for k in range(4) for j in range(2)]
        obse_s[side] = gather_lanes(parts, 16, first).reshape(16, 8, 128)

        @pl.when(y_sides[side][0])
        def _():
            everyone(lambda d: send(obse_s.at[side, d], obse_r.at[1 - side, gz], se_s.at[2, side, 0],
                                    se_r.at[2, 1 - side, 0], {"gy": y_sides[side][1], "gz": d}))

    store_split(xf, toeplitz(px, 31, 256, 512, 8, 8))
    y_forward(yf, py)
    store_split(zf, toeplitz(pz, 61, 128, 256, 34, 1))
    store_split(za, toeplitz(pz, 61, 128, 256, 94, -1))
    store_split(xa, toeplitz(px, 31, 256, 512, 248, -8))
    y_adjoint(ya, py)
    for ref, parts in ((zb, 3), (rb, 2)):
        for part in range(parts):
            ref[part, 0:2] = jnp.zeros((2, 32, 128), F32)
            ref[part, 18:20] = jnp.zeros((2, 32, 128), F32)

    def columns(ref, first, count, c):
        parts = []
        for k in range(TILES):
            groups = [(ref[c, i, :, 8 * k:8 * k + 8, :] if ref.shape[1] < 16 else ref[c, :, i, 8 * k:8 * k + 8, :])
                      .reshape(128, 128) for i in range(first, first + count)]
            parts.append(jnp.concatenate(groups, axis=0))
        return jnp.concatenate(parts, axis=1)

    def tile(value, j):
        return value[:, 128 * j:128 * j + 128]

    def blur_x(matrix, ref, first, c):
        return left_product(matrix, columns(ref, first, 4, c))

    def to_columns(t, value, c):
        parts = [tile(value, k)[128 * j:128 * j + 128] for k in range(TILES) for j in range(2)]
        for k in range(TILES):
            for j in range(2):
                u[t, c, :, j, 8 * k:8 * k + 8, :] = parts[2 * k + j].reshape(16, 8, 128)
        others(lambda d: send(u.at[t, c, d], um.at[t, c, gz], sa_s.at[t, 0], sa_r.at[t, 0, c], {"gz": d}))
        for side, first in ((0, 0), (1, 96)):
            ue_s[t, side, c] = gather_lanes(parts, 32, first).reshape(16, 8, 128)

            @pl.when(y_sides[side][0])
            def _():
                everyone(lambda d: send(ue_s.at[t, side, c, d], ue_r.at[t, 1 - side, c, gz], se_s.at[t, side, c],
                                        se_r.at[t, 1 - side, c], {"gy": y_sides[side][1], "gz": d}))
        um[t, c, gz] = u[t, c, gz]

    def middle(t, own):
        for c in range(CHUNKS):
            z = slice(DEPTH * c, DEPTH * c + DEPTH)
            await_bytes(um.at[t, c, pl.ds(0, 15)], sa_r.at[t, 0, c])
            for side in range(2):
                @pl.when(y_sides[side][0])
                def _():
                    await_bytes(ue_r.at[t, side, c], se_r.at[t, side, c])
            left, right = (ue_r[t, side, c].reshape(128, 128) for side in range(2))
            sides = None
            for j in range(2):
                halo = jnp.concatenate(
                    [spread_lanes(left, right, 32, 2 * k + j).reshape(16, 8, 128) for k in range(TILES)], axis=1)
                own_lanes = um[t, c, :, j].reshape(16 * DEPTH, 128)
                result = right_product(jnp.concatenate([own_lanes, halo.reshape(16 * DEPTH, 128)], axis=1), yf.at[j])
                zb[j, 2:18, z, :] = tile(result, 0).reshape(16, DEPTH, 128)
                sides = tile(result, 1) if sides is None else sides + tile(result, 1)
            zb[2, 2:18, z, :] = sides.reshape(16, DEPTH, 128)
        if t == 0:
            await_bytes(obsb.at[:, :, pl.ds(0, 15)], so_r)
            for side in range(2):
                @pl.when(y_sides[side][0])
                def _():
                    await_bytes(obse_r.at[side], se_r.at[2, side, 0])
            left, right = (obse_r[side].reshape(128, 128) for side in range(2))
            lane = lax.broadcasted_iota(jnp.int32, (128, 128), 1)
            for k in range(4):
                part = spread_lanes(left, right, 32, k)
                obss[:, 8 * k:8 * k + 8, :] = jnp.where(lane < 64, part, 0.0).reshape(16, 8, 128)
        lane = lax.broadcasted_iota(jnp.int32, (128, 128), 1)
        inside = ((lane < 32) & (gy > 0)) | ((lane >= 32) & (lane < 64) & (gy < 3))
        for b in range(4):
            window = jnp.concatenate([zb[j, 4 * b:4 * b + 8].reshape(256, 128) for j in range(3)], axis=1)
            blurred = left_product(zf, window)
            for j in range(2):
                seen = jnp.concatenate([obsb[c, j, 4 * b:4 * b + 4] for c in range(CHUNKS)], axis=1)
                ratios[j, 128 * b:128 * b + 128] = seen.reshape(128, 128) / tile(blurred, j)
            ratio = obss[4 * b:4 * b + 4].reshape(128, 128) / jnp.where(inside, tile(blurred, 2), 1.0)
            ratios[2, 128 * b:128 * b + 128] = jnp.where(inside, ratio, 0.0)
        for j in range(2):
            result = right_product(jnp.concatenate([ratios[j], ratios[2]], axis=1), ya.at[j])
            rb[j, 2:18] = result.reshape(16, 32, 128)

        def far(c, d):
            target = {"gx": 3 - gx, "gz": d}
            if t == 0:
                first = 4 * (gx - 1)

                @pl.when(jnp.logical_not(outer))
                def _():
                    send(wb.at[t, c, d], own.at[c, gz, pl.ds(first, 2)], sf_s.at[t], sf_r.at[t, c], target)

                @pl.when(outer)
                def _():
                    send(wb.at[t, c, d, 2 - gx], own.at[c, gz, first + 2 - gx], sf_s.at[t], sf_r.at[t, c], target)
            else:
                @pl.when(jnp.logical_not(outermost))
                def _():
                    send(wb.at[t, c, d, 2 - gx], own.at[c, gz, 3 * (gx - 1)], sf_s.at[t], sf_r.at[t, c], target)

        def near(c, d):
            send(wb.at[t, c, d], own.at[c, gz, pl.ds(2 - t, 2)], sa_s.at[t, 1], sa_r.at[t, 1, c], {"gz": d})

        for i in range(4):
            b = lax.rem(gz // 4 + (2, 1, 3, 0)[i], 4)
            window = jnp.concatenate([rb[j, pl.ds(4 * b, 8)].reshape(256, 128) for j in range(2)], axis=1)
            back = left_product(za, window)
            for j in range(2):
                result = tile(back, j).reshape(4, 32, 128)
                for c in range(CHUNKS):
                    wb[t, c, pl.ds(4 * b, 4), j] = result[:, DEPTH * c:DEPTH * c + DEPTH]
            for k in range(4):
                d = 4 * b + lax.rem(gz + (2, 1, 3, 0)[k], 4)

                @pl.when(inner)
                def _():
                    far(0, d)
                if i < 3 or k < 3:
                    near(0, d)
        for c in range(1, CHUNKS):
            others(lambda d: near(c, d))

            @pl.when(inner)
            def _():
                everyone(lambda d: far(c, d))
        own[:, gz, 2 - t:4 - t] = wb[t, :, gz]

    def near_copy(t, ref, c):
        if t == 0:
            source, target = ref.at[c, :, pl.ds(2, 2)], ref.at[c, :, pl.ds(4 * parity, 2)]
        else:
            source, target = ref.at[c, :, 2 - parity], ref.at[c, :, 3 * parity]
        return pltpu.make_async_remote_copy(
            src_ref=source, dst_ref=target, send_sem=sn_s.at[t, c], recv_sem=sn_r.at[t, c],
            device_id={"gx": gx + 1 - 2 * parity}, device_id_type=MESH)

    def arrive_own(t, ref, c):
        await_bytes(ref.at[c, pl.ds(0, 15), pl.ds(2 - t, 2)], sa_r.at[t, 1, c])
        near_copy(t, ref, c).start()

    def arrive_halos(t, ref, c):
        near_copy(t, ref, c).wait_recv()

        @pl.when(inner)
        def _():
            await_bytes(ref.at[c, pl.ds(0, 15), pl.ds(0, 2 - t)], sf_r.at[t, c])

    for c in range(CHUNKS):
        for side in range(2):
            @pl.when(x_sides[side][0])
            def _():
                x_copy(1 - side, c).wait_recv()
        to_columns(0, blur_x(xf, obsx, 0, c), c)
    middle(0, wyx0)

    for c in range(CHUNKS):
        arrive_own(0, wyx0, c)
    for c in range(CHUNKS):
        arrive_halos(0, wyx0, c)
        for half in range(2):
            correction = blur_x(xa, wyx0, 2 * half, c)
            new = columns(obsx, 2 * half, 2, c) * correction
            for k in range(TILES):
                est2[c, 2 * half:2 * half + 2, :, 8 * k:8 * k + 8, :] = tile(new, k).reshape(2, 16, 8, 128)
        to_columns(1, blur_x(xf, est2, 0, c), c)
    middle(1, wyx1)

    for c in range(CHUNKS):
        arrive_own(1, wyx1, c)
    for c in range(CHUNKS):
        arrive_halos(1, wyx1, c)
        correction = blur_x(xa, wyx1, 0, c)
        new_estimate = columns(est2, 1, 2, c) * correction
        for k in range(TILES):
            z = slice(DEPTH * c + 8 * k, DEPTH * c + 8 * k + 8)
            new = tile(new_estimate, k).reshape(32, 8, 128)
            for x in range(32):
                est3[32 * x + z.start:32 * x + z.stop] = new[x]
            for x in range(16):
                pooled_z[32 * x + z.start:32 * x + z.stop] = new[2 * x] + new[2 * x + 1]

    halves = pooled_z[pl.ds(0, 256, stride=2), :] + pooled_z[pl.ds(1, 256, stride=2), :]
    for half in range(2):
        pooled_t[half] = jnp.transpose(halves[128 * half:128 * half + 128])
        even, odd = pooled_t[half, pl.ds(0, 64, stride=2), :], pooled_t[half, pl.ds(1, 64, stride=2), :]
        level = (even + odd) * 0.125
        for d in range(16):
            sent_two[d, 4 * half:4 * half + 4] = level[4 * d:4 * d + 4]
    others(lambda d: send(sent_two.at[d], got_two.at[gz], sp_s, sp_r, {"gz": d}))
    got_two[gz] = sent_two[gz]
    for z in range(32):
        est_ref[32 * z:32 * z + 32] = est3[pl.ds(z, 32, stride=32), :]
    await_bytes(got_two.at[pl.ds(0, 15)], sp_r)
    for c in range(CHUNKS):
        for side in range(2):
            @pl.when(x_sides[side][0])
            def _():
                x_copy(side, c).wait_send()

            @pl.when(y_sides[side][0])
            def _():
                for t in range(2):
                    await_bytes(ue_s.at[t, side, c], se_s.at[t, side, c])
        near_copy(0, wyx0, c).wait_send()
        near_copy(1, wyx1, c).wait_send()
    for side in range(2):
        @pl.when(y_sides[side][0])
        def _():
            await_bytes(obse_s.at[side], se_s.at[2, side, 0])

    @pl.when(inner & jnp.logical_not(outer))
    def _():
        await_bytes(wb.at[0], sf_s.at[0])

    @pl.when(outer)
    def _():
        await_bytes(wb.at[0, :, :, 0], sf_s.at[0])

    @pl.when(inner & jnp.logical_not(outermost))
    def _():
        await_bytes(wb.at[1, :, :, 0], sf_s.at[1])
    for t in range(2):
        for way in range(2):
            await_bytes(wb.at[t, :, pl.ds(0, 15)], sa_s.at[t, way])
    await_bytes(obsb.at[:, :, pl.ds(0, 15)], so_s)
    await_bytes(sent_two.at[pl.ds(0, 15)], sp_s)


def finish(est_in, got_two, est_out, two_out, four_out, eight_out, two_ref, four_ref, eight_ref, part_four, sems):
    copies = [pltpu.make_async_copy(a, b, sems.at[i]) for i, (a, b) in enumerate(
        ((est_in, est_out), (two_ref, two_out), (four_ref, four_out), (eight_ref, eight_out)))]
    copies[0].start()
    group = lax.broadcasted_iota(jnp.int32, (8, 128), 1) // 16
    for half in range(2):
        blocks = [got_two[8 * half + s] for s in range(8)]
        for bit in range(3):
            step = 1 << bit
            upper = (group & step) != 0
            for s in range(8):
                if s & step == 0:
                    a, b = blocks[s], blocks[s + step]
                    blocks[s] = jnp.where(upper, pltpu.roll(b, 16 * step, 1), a)
                    blocks[s + step] = jnp.where(upper, b, pltpu.roll(a, 128 - 16 * step, 1))
        for x in range(8):
            two_ref[x, :, 128 * half:128 * half + 128] = blocks[x][0:4]
            two_ref[8 + x, :, 128 * half:128 * half + 128] = blocks[x][4:8]

    copies[1].start()

    def pool_matrix(rows):
        r = lax.broadcasted_iota(jnp.int32, (rows, rows // 2), 0)
        c = lax.broadcasted_iota(jnp.int32, (rows, rows // 2), 1)
        return jnp.where(r // 2 == c, 0.125, 0.0).astype(F32)

    for a in range(8):
        s = two_ref[2 * a] + two_ref[2 * a + 1]
        part_four[2 * a:2 * a + 1] = s[0:1] + s[1:2]
        part_four[2 * a + 1:2 * a + 2] = s[2:3] + s[3:4]
    four = jnp.dot(part_four[...], pool_matrix(256), precision=lax.Precision.HIGHEST, preferred_element_type=F32)
    for a in range(8):
        four_ref[a] = four[2 * a:2 * a + 2]
    rows = [four[4 * a:4 * a + 1] + four[4 * a + 1:4 * a + 2] + four[4 * a + 2:4 * a + 3] + four[4 * a + 3:4 * a + 4]
            for a in range(4)]
    eight = jnp.dot(jnp.concatenate(rows + rows, axis=0), pool_matrix(128),
                    precision=lax.Precision.HIGHEST, preferred_element_type=F32)
    for a in range(4):
        eight_ref[a] = eight[a:a + 1]

    copies[2].start()
    copies[3].start()
    for copy in copies:
        copy.wait()


def shards(observed, profile_x, profile_y, profile_z):
    vmem = pl.BlockSpec(memory_space=pltpu.VMEM)
    smem = pl.BlockSpec(memory_space=pltpu.SMEM)
    dma = pltpu.SemaphoreType.DMA
    estimate, pieces = pl.pallas_call(
        kernel,
        out_shape=[jax.ShapeDtypeStruct((1024, 128), F32), jax.ShapeDtypeStruct((16, 8, 128), F32)],
        in_specs=[pl.BlockSpec(memory_space=pltpu.HBM), smem, smem, smem],
        out_specs=[vmem] * 2,
        scratch_shapes=[
            pltpu.VMEM((1024, 128), F32),
            dma,
            pltpu.VMEM((512, 512), BF16),
            pltpu.VMEM((512, 512), BF16),
            pltpu.VMEM((2, 2, 256, 256), BF16),
            pltpu.VMEM((2, 2, 256, 128), BF16),
            pltpu.VMEM((256, 256), BF16),
            pltpu.VMEM((256, 256), BF16),
            pltpu.VMEM((CHUNKS, 4, 16, DEPTH, 128), F32),
            pltpu.VMEM((CHUNKS, 2, 16, DEPTH, 128), F32),
            pltpu.VMEM((16, 32, 128), F32),
            pltpu.VMEM((2, 16, 8, 128), F32),
            pltpu.VMEM((2, 16, 8, 128), F32),
            pltpu.VMEM((2, CHUNKS, 16, 2, DEPTH, 128), F32),
            pltpu.VMEM((2, CHUNKS, 16, 2, DEPTH, 128), F32),
            pltpu.VMEM((2, 2, CHUNKS, 16, 8, 128), F32),
            pltpu.VMEM((2, 2, CHUNKS, 16, 8, 128), F32),
            pltpu.VMEM((3, 20, 32, 128), F32),
            pltpu.VMEM((3, 512, 128), F32),
            pltpu.VMEM((2, 20, 32, 128), F32),
            pltpu.VMEM((2, CHUNKS, 16, 2, DEPTH, 128), F32),
            pltpu.VMEM((CHUNKS, 16, 6, DEPTH, 128), F32),
            pltpu.VMEM((CHUNKS, 16, 4, DEPTH, 128), F32),
            pltpu.VMEM((CHUNKS, 4, 16, DEPTH, 128), F32),
            pltpu.VMEM((1024, 128), F32),
            pltpu.VMEM((512, 128), F32),
            pltpu.VMEM((2, 128, 128), F32),
            pltpu.VMEM((16, 8, 128), F32),
            dma((2, CHUNKS)), dma((2, CHUNKS)),
            dma((2, CHUNKS)), dma((2, CHUNKS)),
            dma((2,)), dma((2, CHUNKS)),
            dma((3, 2, CHUNKS)), dma((3, 2, CHUNKS)),
            dma((2, 2)), dma((2, 2, CHUNKS)),
            dma, dma, dma, dma,
        ],
        compiler_params=pltpu.CompilerParams(
            collective_id=0, has_side_effects=True, vmem_limit_bytes=48 * 1024 * 1024),
        name="deconvolve",
    )(observed.reshape(1024, 128), profile_x, profile_y, profile_z)
    any_space = pl.BlockSpec(memory_space=pl.ANY)
    estimate, two, four, eight = pl.pallas_call(
        finish,
        out_shape=[
            jax.ShapeDtypeStruct((1024, 128), F32),
            jax.ShapeDtypeStruct((16, 4, 256), F32),
            jax.ShapeDtypeStruct((8, 2, 128), F32),
            jax.ShapeDtypeStruct((4, 1, 64), F32),
        ],
        in_specs=[vmem] * 2,
        out_specs=[any_space] * 4,
        scratch_shapes=[
            pltpu.VMEM((16, 4, 256), F32),
            pltpu.VMEM((8, 2, 128), F32),
            pltpu.VMEM((4, 1, 64), F32),
            pltpu.VMEM((16, 256), F32),
            dma((4,)),
        ],
        compiler_params=pltpu.CompilerParams(vmem_limit_bytes=16 * 1024 * 1024),
        name="pyramid",
    )(estimate, pieces)
    return estimate.reshape(32, 32, 128), two, four, eight


def solution(mesh):
    return jax.shard_map(
        shards,
        mesh=mesh,
        in_specs=(P("gz", "gx", "gy"), P(), P(), P()),
        out_specs=(
            P("gz", "gx", "gy"),
            P("gx", ("gy", "gz"), None),
            P("gx", ("gy", "gz"), None),
            P("gx", ("gy", "gz"), None),
        ),
        check_vma=False,
    )
```

```python
import functools

import jax
import jax.numpy as jnp
from jax import lax
from jax.experimental import pallas as pl
from jax.experimental.pallas import tpu as pltpu
from jax.sharding import PartitionSpec as P

MESH = pl.DeviceIdType.MESH
F32, BF16 = jnp.float32, jnp.bfloat16
CHUNKS = 2
DEPTH = 32 // CHUNKS
TILES = DEPTH // 8


SHIFTS = ((0, 0), (2, 2), (2, 1), (2, 3), (2, 0), (1, 2), (3, 2), (1, 1), (1, 3), (3, 1), (3, 3), (1, 0), (3, 0), (0, 2), (0, 1), (0, 3))


def split(value):
    high = value.astype(BF16)
    return high, (value - high.astype(F32)).astype(BF16)


def dot(a, b):
    return jnp.dot(a, b, preferred_element_type=F32)


def left_product(matrix, value):
    high, low = split(value)
    rows = matrix.shape[0] // 2
    both = dot(matrix[...], high)
    return both[0:rows] + (both[rows:] + dot(matrix[0:rows], low))


def right_product(value, matrix):
    high, low = split(value)
    rows = value.shape[0]
    both = dot(jnp.concatenate([high, low], axis=0), matrix[0])
    return both[0:rows] + (both[rows:] + dot(high, matrix[1]))


def toeplitz(taps, count, rows, width, first, step):
    lane = lax.broadcasted_iota(jnp.int32, (8, width), 1)
    base = jnp.zeros((8, width), F32)
    total = taps[0]
    for s in range(count):
        base = jnp.where(lane == first + step * s, taps[s], base)
        if s:
            total = total + taps[s]
    base = base / jnp.full((8, width), total, F32)
    spread = jnp.broadcast_to(base[0:1], (rows, width))
    return pltpu.roll(spread, 0, 1, stride=1, stride_axis=0)


def store_split(ref, value):
    rows = value.shape[0]
    ref[0:rows], ref[rows:] = split(value)


def y_forward(ref, taps):
    full = toeplitz(taps, 31, 256, 256, 255, -1)
    lane = lax.broadcasted_iota(jnp.int32, (256, 128), 1) // 16
    own = pltpu.roll(full, 240, 1)[:, 0:128]
    for j in range(2):
        left = pltpu.roll(full, 16 * j, 1)[:, 0:128] if j else full[:, 0:128]
        right = pltpu.roll(full, 144 + 16 * j, 1)[:, 0:128]
        side = jnp.where(lane == j, left, jnp.where(lane == 2 + j, right, 0.0))
        for i, part in enumerate(split(jnp.concatenate([own, side], axis=1))):
            ref[j, i, 0:128] = part[32:160]
            ref[j, i, 128:160] = part[0:32]
            ref[j, i, 160:192] = part[160:192]
            ref[j, i, 192:256] = jnp.zeros((64, 256), BF16)


def y_adjoint(ref, taps):
    full = toeplitz(taps, 31, 256, 256, 225, 1)[:, 0:128]
    for i, part in enumerate(split(full)):
        for j in range(2):
            ref[j, i, 128:256] = jnp.zeros((128, 128), BF16)
            ref[j, i, 0:128] = part[16:144]
            ref[j, i, 128 + 16 * j:144 + 16 * j] = part[0:16]
            ref[j, i, 160 + 16 * j:176 + 16 * j] = part[144:160]


def gather_lanes(parts, width, first):
    lane = lax.broadcasted_iota(jnp.int32, parts[0].shape, 1) // width
    result = None
    for k, part in enumerate(parts):
        shift = (width * k - first) % 128
        moved = pltpu.roll(part, shift, 1) if shift else part
        result = moved if result is None else jnp.where(lane == k, moved, result)
    return result


def spread_lanes(left, right, width, k):
    lane = lax.broadcasted_iota(jnp.int32, left.shape, 1)
    a, b = (128 - width * k) % 128, (width - width * k) % 128
    left = pltpu.roll(left, a, 1) if a else left
    right = pltpu.roll(right, b, 1) if b else right
    return jnp.where(lane < width, left, right)


def kernel(obs_hbm, px, py, pz, est_ref, got_two,
           obs_ref, obs_sem, xf, xa, yf, ya, zf, za, obsx, obsb, obss, obse_s, obse_r, u, um, ue_s, ue_r, zb, ratios, rb, wb,
           wyx0, wyx1, est2, est3, pooled_z, pooled_t, sent_two,
           sx_s, sx_r, sn_s, sn_r, sf_s, sf_r, se_s, se_r, sa_s, sa_r, so_s, so_r, sp_s, sp_r):
    gx, gy, gz = lax.axis_index("gx"), lax.axis_index("gy"), lax.axis_index("gz")
    x_sides = ((gx > 0, {"gx": gx - 1}), (gx < 3, {"gx": gx + 1}))
    y_sides = ((gy > 0, gy - 1), (gy < 3, gy + 1))
    inner = (gx == 1) | (gx == 2)
    outermost = ((gx == 1) & (gz == 0)) | ((gx == 2) & (gz == 15))
    outer = ((gx == 1) & (gz < 2)) | ((gx == 2) & (gz > 13))
    parity = lax.rem(gx, 2)

    load = pltpu.make_async_copy(obs_hbm, obs_ref.at[pl.ds(0, 1024)], obs_sem)
    load.start()

    obsx[:, 0, 0] = jnp.zeros((CHUNKS, DEPTH, 128), F32)
    obsx[:, 3, 15] = jnp.zeros((CHUNKS, DEPTH, 128), F32)
    wyx0[:, 0:2, 0] = jnp.zeros((CHUNKS, 2, DEPTH, 128), F32)
    wyx0[:, 14:16, 5] = jnp.zeros((CHUNKS, 2, DEPTH, 128), F32)
    wyx1[:, 0, 0] = jnp.zeros((CHUNKS, DEPTH, 128), F32)
    wyx1[:, 15, 3] = jnp.zeros((CHUNKS, DEPTH, 128), F32)

    @pl.when(gx == 0)
    def _():
        obsx[:, 0] = jnp.zeros((CHUNKS, 16, DEPTH, 128), F32)
        wyx0[:, :, 0:2] = jnp.zeros((CHUNKS, 16, 2, DEPTH, 128), F32)
        wyx1[:, :, 0] = jnp.zeros((CHUNKS, 16, DEPTH, 128), F32)

    @pl.when(gx == 3)
    def _():
        obsx[:, 3] = jnp.zeros((CHUNKS, 16, DEPTH, 128), F32)
        wyx0[:, :, 4:6] = jnp.zeros((CHUNKS, 16, 2, DEPTH, 128), F32)
        wyx1[:, :, 3] = jnp.zeros((CHUNKS, 16, DEPTH, 128), F32)

    for side in range(2):
        @pl.when(jnp.logical_not(y_sides[side][0]))
        def _():
            obse_r[side] = jnp.zeros((16, 8, 128), F32)
            for t in range(2):
                ue_r[t, side] = jnp.zeros((CHUNKS, 16, 8, 128), F32)

    barrier = pltpu.get_barrier_semaphore()

    def greet(target):
        pl.semaphore_signal(barrier, inc=1, device_id=target, device_id_type=MESH)

    def shifted(k, first):
        a, b = SHIFTS[k + first]
        return 4 * lax.rem(gz // 4 + a, 4) + lax.rem(gz + b, 4)

    def others(body):
        for k in range(15):
            body(shifted(k, 1))

    def everyone(body):
        for k in range(16):
            body(shifted((k + 1) % 16, 0))

    greet({"gx": gx + 1 - 2 * parity})

    @pl.when(inner)
    def _():
        everyone(lambda d: greet({"gx": 3 - gx, "gz": d}))
    others(lambda d: greet({"gz": d}))
    for there, target in y_sides:
        @pl.when(there)
        def _():
            everyone(lambda d: greet({"gy": target, "gz": d}))

    load.wait()
    for x in range(32):
        row = obs_ref[pl.ds(x, 32, stride=32), :]
        for c in range(CHUNKS):
            obsx[c, 1 + x // 16, x % 16] = row[DEPTH * c:DEPTH * c + DEPTH]

    neighbours = sum(there.astype(jnp.int32) for there, _ in y_sides) + inner.astype(jnp.int32)
    pl.semaphore_wait(barrier, 16 + 16 * neighbours)

    def await_bytes(ref, sem):
        pltpu.make_async_copy(ref, ref, sem).wait()

    def x_copy(side, c):
        source = obsx.at[c, 1, pl.ds(0, 15)] if side == 0 else obsx.at[c, 2, pl.ds(1, 15)]
        target = obsx.at[c, 3, pl.ds(0, 15)] if side == 0 else obsx.at[c, 0, pl.ds(1, 15)]
        return pltpu.make_async_remote_copy(
            src_ref=source, dst_ref=target, send_sem=sx_s.at[side, c], recv_sem=sx_r.at[side, c],
            device_id=x_sides[side][1], device_id_type=MESH)

    for c in range(CHUNKS):
        for side in range(2):
            @pl.when(x_sides[side][0])
            def _():
                x_copy(side, c).start()

    def send(source, target, send_sem, recv_sem, device):
        pltpu.make_async_remote_copy(
            src_ref=source, dst_ref=target, send_sem=send_sem, recv_sem=recv_sem,
            device_id=device, device_id_type=MESH).start()

    others(lambda d: send(obsx.at[:, pl.ds(1, 2), d], obsb.at[:, :, gz], so_s, so_r, {"gz": d}))
    obsb[:, :, gz] = obsx[:, 1:3, gz]
    for side, first in ((0, 0), (1, 112)):
        parts = [obsx[k // TILES, 1 + j, :, 8 * (k % TILES):8 * (k % TILES) + 8, :].reshape(128, 128)
                 for k in range(4) for j in range(2)]
        obse_s[side] = gather_lanes(parts, 16, first).reshape(16, 8, 128)

        @pl.when(y_sides[side][0])
        def _():
            everyone(lambda d: send(obse_s.at[side, d], obse_r.at[1 - side, gz], se_s.at[2, side, 0],
                                    se_r.at[2, 1 - side, 0], {"gy": y_sides[side][1], "gz": d}))

    store_split(xf, toeplitz(px, 31, 256, 512, 8, 8))
    y_forward(yf, py)
    store_split(zf, toeplitz(pz, 61, 128, 256, 34, 1))
    store_split(za, toeplitz(pz, 61, 128, 256, 94, -1))
    store_split(xa, toeplitz(px, 31, 256, 512, 248, -8))
    y_adjoint(ya, py)
    for ref, parts in ((zb, 3), (rb, 2)):
        for part in range(parts):
            ref[part, 0:2] = jnp.zeros((2, 32, 128), F32)
            ref[part, 18:20] = jnp.zeros((2, 32, 128), F32)

    def columns(ref, first, count, c):
        parts = []
        for k in range(TILES):
            groups = [(ref[c, i, :, 8 * k:8 * k + 8, :] if ref.shape[1] < 16 else ref[c, :, i, 8 * k:8 * k + 8, :])
                      .reshape(128, 128) for i in range(first, first + count)]
            parts.append(jnp.concatenate(groups, axis=0))
        return jnp.concatenate(parts, axis=1)

    def tile(value, j):
        return value[:, 128 * j:128 * j + 128]

    def blur_x(matrix, ref, first, c):
        return left_product(matrix, columns(ref, first, 4, c))

    def to_columns(t, value, c):
        parts = [tile(value, k)[128 * j:128 * j + 128] for k in range(TILES) for j in range(2)]
        for k in range(TILES):
            for j in range(2):
                u[t, c, :, j, 8 * k:8 * k + 8, :] = parts[2 * k + j].reshape(16, 8, 128)
        others(lambda d: send(u.at[t, c, d], um.at[t, c, gz], sa_s.at[t, 0], sa_r.at[t, 0, c], {"gz": d}))
        for side, first in ((0, 0), (1, 96)):
            ue_s[t, side, c] = gather_lanes(parts, 32, first).reshape(16, 8, 128)

            @pl.when(y_sides[side][0])
            def _():
                everyone(lambda d: send(ue_s.at[t, side, c, d], ue_r.at[t, 1 - side, c, gz], se_s.at[t, side, c],
                                        se_r.at[t, 1 - side, c], {"gy": y_sides[side][1], "gz": d}))
        um[t, c, gz] = u[t, c, gz]

    def middle(t, own):
        for c in range(CHUNKS):
            z = slice(DEPTH * c, DEPTH * c + DEPTH)
            await_bytes(um.at[t, c, pl.ds(0, 15)], sa_r.at[t, 0, c])
            for side in range(2):
                @pl.when(y_sides[side][0])
                def _():
                    await_bytes(ue_r.at[t, side, c], se_r.at[t, side, c])
            left, right = (ue_r[t, side, c].reshape(128, 128) for side in range(2))
            sides = None
            for j in range(2):
                halo = jnp.concatenate(
                    [spread_lanes(left, right, 32, 2 * k + j).reshape(16, 8, 128) for k in range(TILES)], axis=1)
                own_lanes = um[t, c, :, j].reshape(16 * DEPTH, 128)
                result = right_product(jnp.concatenate([own_lanes, halo.reshape(16 * DEPTH, 128)], axis=1), yf.at[j])
                zb[j, 2:18, z, :] = tile(result, 0).reshape(16, DEPTH, 128)
                sides = tile(result, 1) if sides is None else sides + tile(result, 1)
            zb[2, 2:18, z, :] = sides.reshape(16, DEPTH, 128)
        if t == 0:
            await_bytes(obsb.at[:, :, pl.ds(0, 15)], so_r)
            for side in range(2):
                @pl.when(y_sides[side][0])
                def _():
                    await_bytes(obse_r.at[side], se_r.at[2, side, 0])
            left, right = (obse_r[side].reshape(128, 128) for side in range(2))
            lane = lax.broadcasted_iota(jnp.int32, (128, 128), 1)
            for k in range(4):
                part = spread_lanes(left, right, 32, k)
                obss[:, 8 * k:8 * k + 8, :] = jnp.where(lane < 64, part, 0.0).reshape(16, 8, 128)
        lane = lax.broadcasted_iota(jnp.int32, (128, 128), 1)
        inside = ((lane < 32) & (gy > 0)) | ((lane >= 32) & (lane < 64) & (gy < 3))
        for b in range(4):
            window = jnp.concatenate([zb[j, 4 * b:4 * b + 8].reshape(256, 128) for j in range(3)], axis=1)
            blurred = left_product(zf, window)
            for j in range(2):
                seen = jnp.concatenate([obsb[c, j, 4 * b:4 * b + 4] for c in range(CHUNKS)], axis=1)
                ratios[j, 128 * b:128 * b + 128] = seen.reshape(128, 128) / tile(blurred, j)
            ratio = obss[4 * b:4 * b + 4].reshape(128, 128) / jnp.where(inside, tile(blurred, 2), 1.0)
            ratios[2, 128 * b:128 * b + 128] = jnp.where(inside, ratio, 0.0)
        for j in range(2):
            result = right_product(jnp.concatenate([ratios[j], ratios[2]], axis=1), ya.at[j])
            rb[j, 2:18] = result.reshape(16, 32, 128)

        def far(c, d):
            target = {"gx": 3 - gx, "gz": d}
            if t == 0:
                first = 4 * (gx - 1)

                @pl.when(jnp.logical_not(outer))
                def _():
                    send(wb.at[t, c, d], own.at[c, gz, pl.ds(first, 2)], sf_s.at[t], sf_r.at[t, c], target)

                @pl.when(outer)
                def _():
                    send(wb.at[t, c, d, 2 - gx], own.at[c, gz, first + 2 - gx], sf_s.at[t], sf_r.at[t, c], target)
            else:
                @pl.when(jnp.logical_not(outermost))
                def _():
                    send(wb.at[t, c, d, 2 - gx], own.at[c, gz, 3 * (gx - 1)], sf_s.at[t], sf_r.at[t, c], target)

        def near(c, d):
            send(wb.at[t, c, d], own.at[c, gz, pl.ds(2 - t, 2)], sa_s.at[t, 1], sa_r.at[t, 1, c], {"gz": d})

        for i in range(4):
            b = lax.rem(gz // 4 + (2, 1, 3, 0)[i], 4)
            window = jnp.concatenate([rb[j, pl.ds(4 * b, 8)].reshape(256, 128) for j in range(2)], axis=1)
            back = left_product(za, window)
            for j in range(2):
                result = tile(back, j).reshape(4, 32, 128)
                for c in range(CHUNKS):
                    wb[t, c, pl.ds(4 * b, 4), j] = result[:, DEPTH * c:DEPTH * c + DEPTH]
            for k in range(4):
                d = 4 * b + lax.rem(gz + (2, 1, 3, 0)[k], 4)

                @pl.when(inner)
                def _():
                    far(0, d)
                if i < 3 or k < 3:
                    near(0, d)
        for c in range(1, CHUNKS):
            others(lambda d: near(c, d))

            @pl.when(inner)
            def _():
                everyone(lambda d: far(c, d))
        own[:, gz, 2 - t:4 - t] = wb[t, :, gz]

    def near_copy(t, ref, c):
        if t == 0:
            source, target = ref.at[c, :, pl.ds(2, 2)], ref.at[c, :, pl.ds(4 * parity, 2)]
        else:
            source, target = ref.at[c, :, 2 - parity], ref.at[c, :, 3 * parity]
        return pltpu.make_async_remote_copy(
            src_ref=source, dst_ref=target, send_sem=sn_s.at[t, c], recv_sem=sn_r.at[t, c],
            device_id={"gx": gx + 1 - 2 * parity}, device_id_type=MESH)

    def arrive_own(t, ref, c):
        await_bytes(ref.at[c, pl.ds(0, 15), pl.ds(2 - t, 2)], sa_r.at[t, 1, c])
        near_copy(t, ref, c).start()

    def arrive_halos(t, ref, c):
        near_copy(t, ref, c).wait_recv()

        @pl.when(inner)
        def _():
            await_bytes(ref.at[c, pl.ds(0, 15), pl.ds(0, 2 - t)], sf_r.at[t, c])

    for c in range(CHUNKS):
        for side in range(2):
            @pl.when(x_sides[side][0])
            def _():
                x_copy(1 - side, c).wait_recv()
        to_columns(0, blur_x(xf, obsx, 0, c), c)
    middle(0, wyx0)

    for c in range(CHUNKS):
        arrive_own(0, wyx0, c)
    for c in range(CHUNKS):
        arrive_halos(0, wyx0, c)
        for half in range(2):
            correction = blur_x(xa, wyx0, 2 * half, c)
            new = columns(obsx, 2 * half, 2, c) * correction
            for k in range(TILES):
                est2[c, 2 * half:2 * half + 2, :, 8 * k:8 * k + 8, :] = tile(new, k).reshape(2, 16, 8, 128)
        to_columns(1, blur_x(xf, est2, 0, c), c)
    middle(1, wyx1)

    for c in range(CHUNKS):
        arrive_own(1, wyx1, c)
    for c in range(CHUNKS):
        arrive_halos(1, wyx1, c)
        correction = blur_x(xa, wyx1, 0, c)
        new_estimate = columns(est2, 1, 2, c) * correction
        for k in range(TILES):
            z = slice(DEPTH * c + 8 * k, DEPTH * c + 8 * k + 8)
            new = tile(new_estimate, k).reshape(32, 8, 128)
            for x in range(32):
                est3[32 * x + z.start:32 * x + z.stop] = new[x]
            for x in range(16):
                pooled_z[32 * x + z.start:32 * x + z.stop] = new[2 * x] + new[2 * x + 1]

    halves = pooled_z[pl.ds(0, 256, stride=2), :] + pooled_z[pl.ds(1, 256, stride=2), :]
    for half in range(2):
        pooled_t[half, 0:128] = jnp.transpose(halves[128 * half:128 * half + 128])
        even, odd = pooled_t[half, pl.ds(0, 64, stride=2), :], pooled_t[half, pl.ds(1, 64, stride=2), :]
        level = (even + odd) * 0.125
        for d in range(16):
            sent_two[d, 4 * half:4 * half + 4] = level[4 * d:4 * d + 4]
    others(lambda d: send(sent_two.at[d], got_two.at[gz], sp_s, sp_r, {"gz": d}))
    got_two[gz] = sent_two[gz]
    for z in range(32):
        est_ref[32 * z:32 * z + 32] = est3[pl.ds(z, 32, stride=32), :]
    await_bytes(got_two.at[pl.ds(0, 15)], sp_r)
    for c in range(CHUNKS):
        for side in range(2):
            @pl.when(x_sides[side][0])
            def _():
                x_copy(side, c).wait_send()

            @pl.when(y_sides[side][0])
            def _():
                for t in range(2):
                    await_bytes(ue_s.at[t, side, c], se_s.at[t, side, c])
        near_copy(0, wyx0, c).wait_send()
        near_copy(1, wyx1, c).wait_send()
    for side in range(2):
        @pl.when(y_sides[side][0])
        def _():
            await_bytes(obse_s.at[side], se_s.at[2, side, 0])

    @pl.when(inner & jnp.logical_not(outer))
    def _():
        await_bytes(wb.at[0], sf_s.at[0])

    @pl.when(outer)
    def _():
        await_bytes(wb.at[0, :, :, 0], sf_s.at[0])

    @pl.when(inner & jnp.logical_not(outermost))
    def _():
        await_bytes(wb.at[1, :, :, 0], sf_s.at[1])
    for t in range(2):
        for way in range(2):
            await_bytes(wb.at[t, :, pl.ds(0, 15)], sa_s.at[t, way])
    await_bytes(obsb.at[:, :, pl.ds(0, 15)], so_s)
    await_bytes(sent_two.at[pl.ds(0, 15)], sp_s)


def finish(est_in, got_two, est_out, two_out, four_out, eight_out, two_ref, four_ref, eight_ref, part_four, sems):
    copies = [pltpu.make_async_copy(a, b, sems.at[i]) for i, (a, b) in enumerate(
        ((est_in, est_out), (two_ref, two_out), (four_ref, four_out), (eight_ref, eight_out)))]
    copies[0].start()
    group = lax.broadcasted_iota(jnp.int32, (8, 128), 1) // 16
    for half in range(2):
        blocks = [got_two[8 * half + s] for s in range(8)]
        for bit in range(3):
            step = 1 << bit
            upper = (group & step) != 0
            for s in range(8):
                if s & step == 0:
                    a, b = blocks[s], blocks[s + step]
                    blocks[s] = jnp.where(upper, pltpu.roll(b, 16 * step, 1), a)
                    blocks[s + step] = jnp.where(upper, b, pltpu.roll(a, 128 - 16 * step, 1))
        for x in range(8):
            two_ref[x, :, 128 * half:128 * half + 128] = blocks[x][0:4]
            two_ref[8 + x, :, 128 * half:128 * half + 128] = blocks[x][4:8]

    copies[1].start()

    def pool_matrix(rows):
        r = lax.broadcasted_iota(jnp.int32, (rows, rows // 2), 0)
        c = lax.broadcasted_iota(jnp.int32, (rows, rows // 2), 1)
        return jnp.where(r // 2 == c, 0.125, 0.0).astype(F32)

    for a in range(8):
        s = two_ref[2 * a] + two_ref[2 * a + 1]
        part_four[2 * a:2 * a + 1] = s[0:1] + s[1:2]
        part_four[2 * a + 1:2 * a + 2] = s[2:3] + s[3:4]
    four = jnp.dot(part_four[...], pool_matrix(256), precision=lax.Precision.HIGHEST, preferred_element_type=F32)
    for a in range(8):
        four_ref[a] = four[2 * a:2 * a + 2]
    rows = [four[4 * a:4 * a + 1] + four[4 * a + 1:4 * a + 2] + four[4 * a + 2:4 * a + 3] + four[4 * a + 3:4 * a + 4]
            for a in range(4)]
    eight = jnp.dot(jnp.concatenate(rows + rows, axis=0), pool_matrix(128),
                    precision=lax.Precision.HIGHEST, preferred_element_type=F32)
    for a in range(4):
        eight_ref[a] = eight[a:a + 1]

    copies[2].start()
    copies[3].start()
    for copy in copies:
        copy.wait()


def shards(observed, profile_x, profile_y, profile_z):
    vmem = pl.BlockSpec(memory_space=pltpu.VMEM)
    smem = pl.BlockSpec(memory_space=pltpu.SMEM)
    dma = pltpu.SemaphoreType.DMA
    estimate, pieces = pl.pallas_call(
        kernel,
        out_shape=[jax.ShapeDtypeStruct((1024, 128), F32), jax.ShapeDtypeStruct((16, 8, 128), F32)],
        in_specs=[pl.BlockSpec(memory_space=pltpu.HBM), smem, smem, smem],
        out_specs=[vmem] * 2,
        scratch_shapes=[
            pltpu.VMEM((1056, 128), F32),
            dma,
            pltpu.VMEM((512, 512), BF16),
            pltpu.VMEM((512, 512), BF16),
            pltpu.VMEM((2, 2, 256, 256), BF16),
            pltpu.VMEM((2, 2, 256, 128), BF16),
            pltpu.VMEM((256, 256), BF16),
            pltpu.VMEM((256, 256), BF16),
            pltpu.VMEM((CHUNKS, 4, 16, DEPTH, 128), F32),
            pltpu.VMEM((CHUNKS, 2, 16, DEPTH, 128), F32),
            pltpu.VMEM((16, 32, 128), F32),
            pltpu.VMEM((2, 16, 8, 128), F32),
            pltpu.VMEM((2, 16, 8, 128), F32),
            pltpu.VMEM((2, CHUNKS, 16, 2, DEPTH, 128), F32),
            pltpu.VMEM((2, CHUNKS, 16, 2, DEPTH, 128), F32),
            pltpu.VMEM((2, 2, CHUNKS, 16, 8, 128), F32),
            pltpu.VMEM((2, 2, CHUNKS, 16, 8, 128), F32),
            pltpu.VMEM((3, 20, 32, 128), F32),
            pltpu.VMEM((3, 512, 128), F32),
            pltpu.VMEM((2, 20, 32, 128), F32),
            pltpu.VMEM((2, CHUNKS, 16, 2, DEPTH, 128), F32),
            pltpu.VMEM((CHUNKS, 16, 6, DEPTH, 128), F32),
            pltpu.VMEM((CHUNKS, 16, 4, DEPTH, 128), F32),
            pltpu.VMEM((CHUNKS, 4, 16, DEPTH, 128), F32),
            pltpu.VMEM((1056, 128), F32),
            pltpu.VMEM((520, 128), F32),
            pltpu.VMEM((2, 136, 128), F32),
            pltpu.VMEM((16, 8, 128), F32),
            dma((2, CHUNKS)), dma((2, CHUNKS)),
            dma((2, CHUNKS)), dma((2, CHUNKS)),
            dma((2,)), dma((2, CHUNKS)),
            dma((3, 2, CHUNKS)), dma((3, 2, CHUNKS)),
            dma((2, 2)), dma((2, 2, CHUNKS)),
            dma, dma, dma, dma,
        ],
        compiler_params=pltpu.CompilerParams(
            collective_id=0, has_side_effects=True, vmem_limit_bytes=48 * 1024 * 1024),
        name="deconvolve",
    )(observed.reshape(1024, 128), profile_x, profile_y, profile_z)
    any_space = pl.BlockSpec(memory_space=pl.ANY)
    estimate, two, four, eight = pl.pallas_call(
        finish,
        out_shape=[
            jax.ShapeDtypeStruct((1024, 128), F32),
            jax.ShapeDtypeStruct((16, 4, 256), F32),
            jax.ShapeDtypeStruct((8, 2, 128), F32),
            jax.ShapeDtypeStruct((4, 1, 64), F32),
        ],
        in_specs=[vmem] * 2,
        out_specs=[any_space] * 4,
        scratch_shapes=[
            pltpu.VMEM((16, 4, 256), F32),
            pltpu.VMEM((8, 2, 128), F32),
            pltpu.VMEM((4, 1, 64), F32),
            pltpu.VMEM((16, 256), F32),
            dma((4,)),
        ],
        compiler_params=pltpu.CompilerParams(vmem_limit_bytes=16 * 1024 * 1024),
        name="pyramid",
    )(estimate, pieces)
    return estimate.reshape(32, 32, 128), two, four, eight


def solution(mesh):
    return jax.shard_map(
        shards,
        mesh=mesh,
        in_specs=(P("gz", "gx", "gy"), P(), P(), P()),
        out_specs=(
            P("gz", "gx", "gy"),
            P("gx", ("gy", "gz"), None),
            P("gx", ("gy", "gz"), None),
            P("gx", ("gy", "gz"), None),
        ),
        check_vma=False,
    )
```

```python
import functools

import jax
import jax.numpy as jnp
from jax import lax
from jax.experimental import pallas as pl
from jax.experimental.pallas import tpu as pltpu
from jax.sharding import PartitionSpec as P

MESH = pl.DeviceIdType.MESH
F32, BF16 = jnp.float32, jnp.bfloat16
CHUNKS = 2
DEPTH = 32 // CHUNKS
TILES = DEPTH // 8


SHIFTS = ((0, 0), (2, 2), (2, 1), (2, 3), (2, 0), (1, 2), (3, 2), (1, 1), (1, 3), (3, 1), (3, 3), (1, 0), (3, 0), (0, 2), (0, 1), (0, 3))


def split(value):
    high = value.astype(BF16)
    return high, (value - high.astype(F32)).astype(BF16)


def dot(a, b):
    return jnp.dot(a, b, preferred_element_type=F32)


def left_product(matrix, value):
    high, low = split(value)
    rows = matrix.shape[0] // 2
    both = dot(matrix[...], high)
    return both[0:rows] + (both[rows:] + dot(matrix[0:rows], low))


def right_product(value, matrix):
    high, low = split(value)
    rows = value.shape[0]
    both = dot(jnp.concatenate([high, low], axis=0), matrix[0])
    return both[0:rows] + (both[rows:] + dot(high, matrix[1]))


def toeplitz(taps, count, rows, width, first, step):
    lane = lax.broadcasted_iota(jnp.int32, (8, width), 1)
    base = jnp.zeros((8, width), F32)
    total = taps[0]
    for s in range(count):
        base = jnp.where(lane == first + step * s, taps[s], base)
        if s:
            total = total + taps[s]
    base = base / jnp.full((8, width), total, F32)
    spread = jnp.broadcast_to(base[0:1], (rows, width))
    return pltpu.roll(spread, 0, 1, stride=1, stride_axis=0)


def store_split(ref, value):
    rows = value.shape[0]
    ref[0:rows], ref[rows:] = split(value)


def y_forward(ref, taps):
    full = toeplitz(taps, 31, 256, 256, 255, -1)
    lane = lax.broadcasted_iota(jnp.int32, (256, 128), 1) // 16
    own = pltpu.roll(full, 240, 1)[:, 0:128]
    for j in range(2):
        left = pltpu.roll(full, 16 * j, 1)[:, 0:128] if j else full[:, 0:128]
        right = pltpu.roll(full, 144 + 16 * j, 1)[:, 0:128]
        side = jnp.where(lane == j, left, jnp.where(lane == 2 + j, right, 0.0))
        for i, part in enumerate(split(jnp.concatenate([own, side], axis=1))):
            ref[j, i, 0:128] = part[32:160]
            ref[j, i, 128:160] = part[0:32]
            ref[j, i, 160:192] = part[160:192]
            ref[j, i, 192:256] = jnp.zeros((64, 256), BF16)


def y_adjoint(ref, taps):
    full = toeplitz(taps, 31, 256, 256, 225, 1)[:, 0:128]
    for i, part in enumerate(split(full)):
        for j in range(2):
            ref[j, i, 128:256] = jnp.zeros((128, 128), BF16)
            ref[j, i, 0:128] = part[16:144]
            ref[j, i, 128 + 16 * j:144 + 16 * j] = part[0:16]
            ref[j, i, 160 + 16 * j:176 + 16 * j] = part[144:160]


def gather_lanes(parts, width, first):
    lane = lax.broadcasted_iota(jnp.int32, parts[0].shape, 1) // width
    result = None
    for k, part in enumerate(parts):
        shift = (width * k - first) % 128
        moved = pltpu.roll(part, shift, 1) if shift else part
        result = moved if result is None else jnp.where(lane == k, moved, result)
    return result


def spread_lanes(left, right, width, k):
    lane = lax.broadcasted_iota(jnp.int32, left.shape, 1)
    a, b = (128 - width * k) % 128, (width - width * k) % 128
    left = pltpu.roll(left, a, 1) if a else left
    right = pltpu.roll(right, b, 1) if b else right
    return jnp.where(lane < width, left, right)


def kernel(obs_hbm, px, py, pz, est_ref, got_two,
           obs_ref, obs_sem, xf, xa, yf, ya, zf, za, obsx, obsb, obss, obse_s, obse_r, u, um, ue_s, ue_r, zb, ratios, rb, wb,
           wyx0, wyx1, est2, est3, pooled_z, pooled_t, sent_two,
           sx_s, sx_r, sn_s, sn_r, sf_s, sf_r, se_s, se_r, sa_s, sa_r, so_s, so_r, sp_s, sp_r):
    gx, gy, gz = lax.axis_index("gx"), lax.axis_index("gy"), lax.axis_index("gz")
    x_sides = ((gx > 0, {"gx": gx - 1}), (gx < 3, {"gx": gx + 1}))
    y_sides = ((gy > 0, gy - 1), (gy < 3, gy + 1))
    inner = (gx == 1) | (gx == 2)
    outermost = ((gx == 1) & (gz == 0)) | ((gx == 2) & (gz == 15))
    outer = ((gx == 1) & (gz < 2)) | ((gx == 2) & (gz > 13))
    parity = lax.rem(gx, 2)

    load = pltpu.make_async_copy(obs_hbm, obs_ref.at[pl.ds(0, 1024)], obs_sem)
    load.start()

    obsx[:, 0, 0] = jnp.zeros((CHUNKS, DEPTH, 128), F32)
    obsx[:, 3, 15] = jnp.zeros((CHUNKS, DEPTH, 128), F32)
    wyx0[:, 0:2, 0] = jnp.zeros((CHUNKS, 2, DEPTH, 128), F32)
    wyx0[:, 14:16, 5] = jnp.zeros((CHUNKS, 2, DEPTH, 128), F32)
    wyx1[:, 0, 0] = jnp.zeros((CHUNKS, DEPTH, 128), F32)
    wyx1[:, 15, 3] = jnp.zeros((CHUNKS, DEPTH, 128), F32)

    @pl.when(gx == 0)
    def _():
        obsx[:, 0] = jnp.zeros((CHUNKS, 16, DEPTH, 128), F32)
        wyx0[:, :, 0:2] = jnp.zeros((CHUNKS, 16, 2, DEPTH, 128), F32)
        wyx1[:, :, 0] = jnp.zeros((CHUNKS, 16, DEPTH, 128), F32)

    @pl.when(gx == 3)
    def _():
        obsx[:, 3] = jnp.zeros((CHUNKS, 16, DEPTH, 128), F32)
        wyx0[:, :, 4:6] = jnp.zeros((CHUNKS, 16, 2, DEPTH, 128), F32)
        wyx1[:, :, 3] = jnp.zeros((CHUNKS, 16, DEPTH, 128), F32)

    for side in range(2):
        @pl.when(jnp.logical_not(y_sides[side][0]))
        def _():
            obse_r[side] = jnp.zeros((16, 8, 128), F32)
            for t in range(2):
                ue_r[t, side] = jnp.zeros((CHUNKS, 16, 8, 128), F32)

    barrier = pltpu.get_barrier_semaphore()

    def greet(target):
        pl.semaphore_signal(barrier, inc=1, device_id=target, device_id_type=MESH)

    def shifted(k, first):
        a, b = SHIFTS[k + first]
        return 4 * lax.rem(gz // 4 + a, 4) + lax.rem(gz + b, 4)

    def others(body):
        for k in range(15):
            body(shifted(k, 1))

    def everyone(body):
        for k in range(16):
            body(shifted((k + 1) % 16, 0))

    greet({"gx": gx + 1 - 2 * parity})

    @pl.when(inner)
    def _():
        everyone(lambda d: greet({"gx": 3 - gx, "gz": d}))
    others(lambda d: greet({"gz": d}))
    for there, target in y_sides:
        @pl.when(there)
        def _():
            everyone(lambda d: greet({"gy": target, "gz": d}))

    load.wait()
    for x in range(32):
        row = obs_ref[pl.ds(x, 32, stride=32), :]
        for c in range(CHUNKS):
            obsx[c, 1 + x // 16, x % 16] = row[DEPTH * c:DEPTH * c + DEPTH]

    neighbours = sum(there.astype(jnp.int32) for there, _ in y_sides) + inner.astype(jnp.int32)
    pl.semaphore_wait(barrier, 16 + 16 * neighbours)

    def await_bytes(ref, sem):
        pltpu.make_async_copy(ref, ref, sem).wait()

    def x_copy(side, c):
        source = obsx.at[c, 1, pl.ds(0, 15)] if side == 0 else obsx.at[c, 2, pl.ds(1, 15)]
        target = obsx.at[c, 3, pl.ds(0, 15)] if side == 0 else obsx.at[c, 0, pl.ds(1, 15)]
        return pltpu.make_async_remote_copy(
            src_ref=source, dst_ref=target, send_sem=sx_s.at[side, c], recv_sem=sx_r.at[side, c],
            device_id=x_sides[side][1], device_id_type=MESH)

    for c in range(CHUNKS):
        for side in range(2):
            @pl.when(x_sides[side][0])
            def _():
                x_copy(side, c).start()

    def send(source, target, send_sem, recv_sem, device):
        pltpu.make_async_remote_copy(
            src_ref=source, dst_ref=target, send_sem=send_sem, recv_sem=recv_sem,
            device_id=device, device_id_type=MESH).start()

    others(lambda d: send(obsx.at[:, pl.ds(1, 2), d], obsb.at[:, :, gz], so_s, so_r, {"gz": d}))
    obsb[:, :, gz] = obsx[:, 1:3, gz]
    for side, first in ((0, 0), (1, 112)):
        parts = [obsx[k // TILES, 1 + j, :, 8 * (k % TILES):8 * (k % TILES) + 8, :].reshape(128, 128)
                 for k in range(4) for j in range(2)]
        obse_s[side] = gather_lanes(parts, 16, first).reshape(16, 8, 128)

        @pl.when(y_sides[side][0])
        def _():
            everyone(lambda d: send(obse_s.at[side, d], obse_r.at[1 - side, gz], se_s.at[2, side, 0],
                                    se_r.at[2, 1 - side, 0], {"gy": y_sides[side][1], "gz": d}))

    store_split(xf, toeplitz(px, 31, 256, 512, 8, 8))
    y_forward(yf, py)
    store_split(zf, toeplitz(pz, 61, 128, 256, 34, 1))
    store_split(za, toeplitz(pz, 61, 128, 256, 94, -1))
    store_split(xa, toeplitz(px, 31, 256, 512, 248, -8))
    y_adjoint(ya, py)
    for ref, parts in ((zb, 3), (rb, 2)):
        for part in range(parts):
            ref[part, 0:2] = jnp.zeros((2, 32, 128), F32)
            ref[part, 18:20] = jnp.zeros((2, 32, 128), F32)

    def columns(ref, first, count, c):
        parts = []
        for k in range(TILES):
            groups = [(ref[c, i, :, 8 * k:8 * k + 8, :] if ref.shape[1] < 16 else ref[c, :, i, 8 * k:8 * k + 8, :])
                      .reshape(128, 128) for i in range(first, first + count)]
            parts.append(jnp.concatenate(groups, axis=0))
        return jnp.concatenate(parts, axis=1)

    def tile(value, j):
        return value[:, 128 * j:128 * j + 128]

    def blur_x(matrix, ref, first, c):
        return left_product(matrix, columns(ref, first, 4, c))

    def to_columns(t, value, c):
        parts = [tile(value, k)[128 * j:128 * j + 128] for k in range(TILES) for j in range(2)]
        for k in range(TILES):
            for j in range(2):
                u[t, c, :, j, 8 * k:8 * k + 8, :] = parts[2 * k + j].reshape(16, 8, 128)
        others(lambda d: send(u.at[t, c, d], um.at[t, c, gz], sa_s.at[t, 0], sa_r.at[t, 0, c], {"gz": d}))
        for side, first in ((0, 0), (1, 96)):
            ue_s[t, side, c] = gather_lanes(parts, 32, first).reshape(16, 8, 128)

            @pl.when(y_sides[side][0])
            def _():
                everyone(lambda d: send(ue_s.at[t, side, c, d], ue_r.at[t, 1 - side, c, gz], se_s.at[t, side, c],
                                        se_r.at[t, 1 - side, c], {"gy": y_sides[side][1], "gz": d}))
        um[t, c, gz] = u[t, c, gz]

    def middle(t, own):
        for c in range(CHUNKS):
            if t == 0 and c == CHUNKS - 1:
                await_bytes(obsb.at[:, :, pl.ds(0, 15)], so_r)
                for side in range(2):
                    @pl.when(y_sides[side][0])
                    def _():
                        await_bytes(obse_r.at[side], se_r.at[2, side, 0])
                left, right = (obse_r[side].reshape(128, 128) for side in range(2))
                lane = lax.broadcasted_iota(jnp.int32, (128, 128), 1)
                for k in range(4):
                    part = spread_lanes(left, right, 32, k)
                    obss[:, 8 * k:8 * k + 8, :] = jnp.where(lane < 64, part, 0.0).reshape(16, 8, 128)
            z = slice(DEPTH * c, DEPTH * c + DEPTH)
            await_bytes(um.at[t, c, pl.ds(0, 15)], sa_r.at[t, 0, c])
            for side in range(2):
                @pl.when(y_sides[side][0])
                def _():
                    await_bytes(ue_r.at[t, side, c], se_r.at[t, side, c])
            left, right = (ue_r[t, side, c].reshape(128, 128) for side in range(2))
            sides = None
            for j in range(2):
                halo = jnp.concatenate(
                    [spread_lanes(left, right, 32, 2 * k + j).reshape(16, 8, 128) for k in range(TILES)], axis=1)
                own_lanes = um[t, c, :, j].reshape(16 * DEPTH, 128)
                result = right_product(jnp.concatenate([own_lanes, halo.reshape(16 * DEPTH, 128)], axis=1), yf.at[j])
                zb[j, 2:18, z, :] = tile(result, 0).reshape(16, DEPTH, 128)
                sides = tile(result, 1) if sides is None else sides + tile(result, 1)
            zb[2, 2:18, z, :] = sides.reshape(16, DEPTH, 128)
        lane = lax.broadcasted_iota(jnp.int32, (128, 128), 1)
        inside = ((lane < 32) & (gy > 0)) | ((lane >= 32) & (lane < 64) & (gy < 3))
        for b in range(4):
            window = jnp.concatenate([zb[j, 4 * b:4 * b + 8].reshape(256, 128) for j in range(3)], axis=1)
            blurred = left_product(zf, window)
            for j in range(2):
                seen = jnp.concatenate([obsb[c, j, 4 * b:4 * b + 4] for c in range(CHUNKS)], axis=1)
                ratios[j, 128 * b:128 * b + 128] = seen.reshape(128, 128) / tile(blurred, j)
            ratio = obss[4 * b:4 * b + 4].reshape(128, 128) / jnp.where(inside, tile(blurred, 2), 1.0)
            ratios[2, 128 * b:128 * b + 128] = jnp.where(inside, ratio, 0.0)
        for j in range(2):
            result = right_product(jnp.concatenate([ratios[j], ratios[2]], axis=1), ya.at[j])
            rb[j, 2:18] = result.reshape(16, 32, 128)

        def far(c, d):
            target = {"gx": 3 - gx, "gz": d}
            if t == 0:
                first = 4 * (gx - 1)

                @pl.when(jnp.logical_not(outer))
                def _():
                    send(wb.at[t, c, d], own.at[c, gz, pl.ds(first, 2)], sf_s.at[t], sf_r.at[t, c], target)

                @pl.when(outer)
                def _():
                    send(wb.at[t, c, d, 2 - gx], own.at[c, gz, first + 2 - gx], sf_s.at[t], sf_r.at[t, c], target)
            else:
                @pl.when(jnp.logical_not(outermost))
                def _():
                    send(wb.at[t, c, d, 2 - gx], own.at[c, gz, 3 * (gx - 1)], sf_s.at[t], sf_r.at[t, c], target)

        def near(c, d):
            send(wb.at[t, c, d], own.at[c, gz, pl.ds(2 - t, 2)], sa_s.at[t, 1], sa_r.at[t, 1, c], {"gz": d})

        for i in range(4):
            b = lax.rem(gz // 4 + (2, 1, 3, 0)[i], 4)
            window = jnp.concatenate([rb[j, pl.ds(4 * b, 8)].reshape(256, 128) for j in range(2)], axis=1)
            back = left_product(za, window)
            for j in range(2):
                result = tile(back, j).reshape(4, 32, 128)
                for c in range(CHUNKS):
                    wb[t, c, pl.ds(4 * b, 4), j] = result[:, DEPTH * c:DEPTH * c + DEPTH]
            for k in range(4):
                d = 4 * b + lax.rem(gz + (2, 1, 3, 0)[k], 4)

                @pl.when(inner)
                def _():
                    far(0, d)
                if i < 3 or k < 3:
                    near(0, d)
        for c in range(1, CHUNKS):
            others(lambda d: near(c, d))

            @pl.when(inner)
            def _():
                everyone(lambda d: far(c, d))
        own[:, gz, 2 - t:4 - t] = wb[t, :, gz]

    def near_copy(t, ref, c):
        if t == 0:
            source, target = ref.at[c, :, pl.ds(2, 2)], ref.at[c, :, pl.ds(4 * parity, 2)]
        else:
            source, target = ref.at[c, :, 2 - parity], ref.at[c, :, 3 * parity]
        return pltpu.make_async_remote_copy(
            src_ref=source, dst_ref=target, send_sem=sn_s.at[t, c], recv_sem=sn_r.at[t, c],
            device_id={"gx": gx + 1 - 2 * parity}, device_id_type=MESH)

    def arrive_own(t, ref, c):
        await_bytes(ref.at[c, pl.ds(0, 15), pl.ds(2 - t, 2)], sa_r.at[t, 1, c])
        near_copy(t, ref, c).start()

    def arrive_halos(t, ref, c):
        near_copy(t, ref, c).wait_recv()

        @pl.when(inner)
        def _():
            await_bytes(ref.at[c, pl.ds(0, 15), pl.ds(0, 2 - t)], sf_r.at[t, c])

    for c in range(CHUNKS):
        for side in range(2):
            @pl.when(x_sides[side][0])
            def _():
                x_copy(1 - side, c).wait_recv()
        to_columns(0, blur_x(xf, obsx, 0, c), c)
    middle(0, wyx0)

    for c in range(CHUNKS):
        arrive_own(0, wyx0, c)
    for c in range(CHUNKS):
        arrive_halos(0, wyx0, c)
        for half in range(2):
            correction = blur_x(xa, wyx0, 2 * half, c)
            new = columns(obsx, 2 * half, 2, c) * correction
            for k in range(TILES):
                est2[c, 2 * half:2 * half + 2, :, 8 * k:8 * k + 8, :] = tile(new, k).reshape(2, 16, 8, 128)
        to_columns(1, blur_x(xf, est2, 0, c), c)
    middle(1, wyx1)

    for c in range(CHUNKS):
        arrive_own(1, wyx1, c)
    for c in range(CHUNKS):
        arrive_halos(1, wyx1, c)
        correction = blur_x(xa, wyx1, 0, c)
        new_estimate = columns(est2, 1, 2, c) * correction
        for k in range(TILES):
            z = slice(DEPTH * c + 8 * k, DEPTH * c + 8 * k + 8)
            new = tile(new_estimate, k).reshape(32, 8, 128)
            for x in range(32):
                est3[32 * x + z.start:32 * x + z.stop] = new[x]
            for x in range(16):
                pooled_z[32 * x + z.start:32 * x + z.stop] = new[2 * x] + new[2 * x + 1]

    halves = pooled_z[pl.ds(0, 256, stride=2), :] + pooled_z[pl.ds(1, 256, stride=2), :]
    for half in range(2):
        pooled_t[half, 0:128] = jnp.transpose(halves[128 * half:128 * half + 128])
        even, odd = pooled_t[half, pl.ds(0, 64, stride=2), :], pooled_t[half, pl.ds(1, 64, stride=2), :]
        level = (even + odd) * 0.125
        for d in range(16):
            sent_two[d, 4 * half:4 * half + 4] = level[4 * d:4 * d + 4]
    others(lambda d: send(sent_two.at[d], got_two.at[gz], sp_s, sp_r, {"gz": d}))
    got_two[gz] = sent_two[gz]
    for z in range(32):
        est_ref[32 * z:32 * z + 32] = est3[pl.ds(z, 32, stride=32), :]
    await_bytes(got_two.at[pl.ds(0, 15)], sp_r)
    for c in range(CHUNKS):
        for side in range(2):
            @pl.when(x_sides[side][0])
            def _():
                x_copy(side, c).wait_send()

            @pl.when(y_sides[side][0])
            def _():
                for t in range(2):
                    await_bytes(ue_s.at[t, side, c], se_s.at[t, side, c])
        near_copy(0, wyx0, c).wait_send()
        near_copy(1, wyx1, c).wait_send()
    for side in range(2):
        @pl.when(y_sides[side][0])
        def _():
            await_bytes(obse_s.at[side], se_s.at[2, side, 0])

    @pl.when(inner & jnp.logical_not(outer))
    def _():
        await_bytes(wb.at[0], sf_s.at[0])

    @pl.when(outer)
    def _():
        await_bytes(wb.at[0, :, :, 0], sf_s.at[0])

    @pl.when(inner & jnp.logical_not(outermost))
    def _():
        await_bytes(wb.at[1, :, :, 0], sf_s.at[1])
    for t in range(2):
        for way in range(2):
            await_bytes(wb.at[t, :, pl.ds(0, 15)], sa_s.at[t, way])
    await_bytes(obsb.at[:, :, pl.ds(0, 15)], so_s)
    await_bytes(sent_two.at[pl.ds(0, 15)], sp_s)


def finish(est_in, got_two, est_out, two_out, four_out, eight_out, two_ref, four_ref, eight_ref, part_four, sems):
    copies = [pltpu.make_async_copy(a, b, sems.at[i]) for i, (a, b) in enumerate(
        ((est_in, est_out), (two_ref, two_out), (four_ref, four_out), (eight_ref, eight_out)))]
    copies[0].start()
    group = lax.broadcasted_iota(jnp.int32, (8, 128), 1) // 16
    for half in range(2):
        blocks = [got_two[8 * half + s] for s in range(8)]
        for bit in range(3):
            step = 1 << bit
            upper = (group & step) != 0
            for s in range(8):
                if s & step == 0:
                    a, b = blocks[s], blocks[s + step]
                    blocks[s] = jnp.where(upper, pltpu.roll(b, 16 * step, 1), a)
                    blocks[s + step] = jnp.where(upper, b, pltpu.roll(a, 128 - 16 * step, 1))
        for x in range(8):
            two_ref[x, :, 128 * half:128 * half + 128] = blocks[x][0:4]
            two_ref[8 + x, :, 128 * half:128 * half + 128] = blocks[x][4:8]

    copies[1].start()

    def pool_matrix(rows):
        r = lax.broadcasted_iota(jnp.int32, (rows, rows // 2), 0)
        c = lax.broadcasted_iota(jnp.int32, (rows, rows // 2), 1)
        return jnp.where(r // 2 == c, 0.125, 0.0).astype(F32)

    for a in range(8):
        s = two_ref[2 * a] + two_ref[2 * a + 1]
        part_four[2 * a:2 * a + 1] = s[0:1] + s[1:2]
        part_four[2 * a + 1:2 * a + 2] = s[2:3] + s[3:4]
    four = jnp.dot(part_four[...], pool_matrix(256), precision=lax.Precision.HIGHEST, preferred_element_type=F32)
    for a in range(8):
        four_ref[a] = four[2 * a:2 * a + 2]
    rows = [four[4 * a:4 * a + 1] + four[4 * a + 1:4 * a + 2] + four[4 * a + 2:4 * a + 3] + four[4 * a + 3:4 * a + 4]
            for a in range(4)]
    eight = jnp.dot(jnp.concatenate(rows + rows, axis=0), pool_matrix(128),
                    precision=lax.Precision.HIGHEST, preferred_element_type=F32)
    for a in range(4):
        eight_ref[a] = eight[a:a + 1]

    copies[2].start()
    copies[3].start()
    for copy in copies:
        copy.wait()


def shards(observed, profile_x, profile_y, profile_z):
    vmem = pl.BlockSpec(memory_space=pltpu.VMEM)
    smem = pl.BlockSpec(memory_space=pltpu.SMEM)
    dma = pltpu.SemaphoreType.DMA
    estimate, pieces = pl.pallas_call(
        kernel,
        out_shape=[jax.ShapeDtypeStruct((1024, 128), F32), jax.ShapeDtypeStruct((16, 8, 128), F32)],
        in_specs=[pl.BlockSpec(memory_space=pltpu.HBM), smem, smem, smem],
        out_specs=[vmem] * 2,
        scratch_shapes=[
            pltpu.VMEM((1056, 128), F32),
            dma,
            pltpu.VMEM((512, 512), BF16),
            pltpu.VMEM((512, 512), BF16),
            pltpu.VMEM((2, 2, 256, 256), BF16),
            pltpu.VMEM((2, 2, 256, 128), BF16),
            pltpu.VMEM((256, 256), BF16),
            pltpu.VMEM((256, 256), BF16),
            pltpu.VMEM((CHUNKS, 4, 16, DEPTH, 128), F32),
            pltpu.VMEM((CHUNKS, 2, 16, DEPTH, 128), F32),
            pltpu.VMEM((16, 32, 128), F32),
            pltpu.VMEM((2, 16, 8, 128), F32),
            pltpu.VMEM((2, 16, 8, 128), F32),
            pltpu.VMEM((2, CHUNKS, 16, 2, DEPTH, 128), F32),
            pltpu.VMEM((2, CHUNKS, 16, 2, DEPTH, 128), F32),
            pltpu.VMEM((2, 2, CHUNKS, 16, 8, 128), F32),
            pltpu.VMEM((2, 2, CHUNKS, 16, 8, 128), F32),
            pltpu.VMEM((3, 20, 32, 128), F32),
            pltpu.VMEM((3, 512, 128), F32),
            pltpu.VMEM((2, 20, 32, 128), F32),
            pltpu.VMEM((2, CHUNKS, 16, 2, DEPTH, 128), F32),
            pltpu.VMEM((CHUNKS, 16, 6, DEPTH, 128), F32),
            pltpu.VMEM((CHUNKS, 16, 4, DEPTH, 128), F32),
            pltpu.VMEM((CHUNKS, 4, 16, DEPTH, 128), F32),
            pltpu.VMEM((1056, 128), F32),
            pltpu.VMEM((520, 128), F32),
            pltpu.VMEM((2, 136, 128), F32),
            pltpu.VMEM((16, 8, 128), F32),
            dma((2, CHUNKS)), dma((2, CHUNKS)),
            dma((2, CHUNKS)), dma((2, CHUNKS)),
            dma((2,)), dma((2, CHUNKS)),
            dma((3, 2, CHUNKS)), dma((3, 2, CHUNKS)),
            dma((2, 2)), dma((2, 2, CHUNKS)),
            dma, dma, dma, dma,
        ],
        compiler_params=pltpu.CompilerParams(
            collective_id=0, has_side_effects=True, vmem_limit_bytes=48 * 1024 * 1024),
        name="deconvolve",
    )(observed.reshape(1024, 128), profile_x, profile_y, profile_z)
    any_space = pl.BlockSpec(memory_space=pl.ANY)
    estimate, two, four, eight = pl.pallas_call(
        finish,
        out_shape=[
            jax.ShapeDtypeStruct((1024, 128), F32),
            jax.ShapeDtypeStruct((16, 4, 256), F32),
            jax.ShapeDtypeStruct((8, 2, 128), F32),
            jax.ShapeDtypeStruct((4, 1, 64), F32),
        ],
        in_specs=[vmem] * 2,
        out_specs=[any_space] * 4,
        scratch_shapes=[
            pltpu.VMEM((16, 4, 256), F32),
            pltpu.VMEM((8, 2, 128), F32),
            pltpu.VMEM((4, 1, 64), F32),
            pltpu.VMEM((16, 256), F32),
            dma((4,)),
        ],
        compiler_params=pltpu.CompilerParams(vmem_limit_bytes=16 * 1024 * 1024),
        name="pyramid",
    )(estimate, pieces)
    return estimate.reshape(32, 32, 128), two, four, eight


def solution(mesh):
    return jax.shard_map(
        shards,
        mesh=mesh,
        in_specs=(P("gz", "gx", "gy"), P(), P(), P()),
        out_specs=(
            P("gz", "gx", "gy"),
            P("gx", ("gy", "gz"), None),
            P("gx", ("gy", "gz"), None),
            P("gx", ("gy", "gz"), None),
        ),
        check_vma=False,
    )
```
